256 devices in a mesh: seqhi: 8 (over x, core), seqlo: 32 (over y, z).
Axes of the slice: x: 4, y: 4, z: 8, core: 2. Of those that a mesh axis runs over, the one named last changes fastest.
Arguments:
- queries: float32 [32768, 768], P(('seqhi', 'seqlo')), may hold values from -6 to 6
- keys: float32 [32768, 768], P(('seqhi', 'seqlo')), may hold values from -6 to 6
- values: float32 [32768, 768], P(('seqhi', 'seqlo')), may hold values from -6 to 6
- cotangent: float32 [32768, 768], P(('seqhi', 'seqlo')), may hold values from -6 to 6
Outputs:
- attended: float32 [32768, 768], P(('seqhi', 'seqlo'))
- query_grad: float32 [32768, 768], P(('seqhi', 'seqlo'))
- key_grad: float32 [32768, 768], P(('seqhi', 'seqlo'))
- value_grad: float32 [32768, 768], P(('seqhi', 'seqlo'))
The draws below stay inside these ranges and needn't reach their ends.
All inputs are finite; a program needn't handle non-finite values.
Results may differ from the reference program's by a relative error of at most 0.0003.
Values sent between devices are 32-bit elements; how exact they have to be, the bound alone decides.
A program may use at most 128 MiB of HBM per device.

```python
import math
import jax
import jax.numpy as jnp
from jax import lax

HEADS = 12
D = 768
BLOCK = 128
TOKENS = 32768


def draw_queries(key, part):
    key = jax.random.fold_in(key, 1)
    return jnp.clip(jax.random.normal(key, (TOKENS, D), jnp.float32), -6.0, 6.0)


def draw_keys(key, part):
    key = jax.random.fold_in(key, 2)
    return jnp.clip(jax.random.normal(key, (TOKENS, D), jnp.float32), -6.0, 6.0)


def block_levels(own_key, dims, cuts, low, high):
    factor_of = 1.0
    for dim, blocks in cuts:
        heights = jax.random.uniform(jax.random.fold_in(jax.random.fold_in(own_key, 6), dim), (blocks,), jnp.float32, low / len(cuts), high / len(cuts))
        factor_of = factor_of * jnp.repeat(jnp.exp(heights), dims[dim] // blocks).reshape((-1,) + (1,) * (len(dims) - 1 - dim))
    return factor_of


def centred(rng, dims, width, bound, pieces=(), held_as=jnp.bfloat16):
    entries = width * jax.random.normal(rng, dims, jnp.float32)
    if pieces:
        entries = entries * block_levels(rng, dims, pieces, -0.22, 0.18)
    return jnp.clip(entries, -bound, bound).astype(held_as)


def setup_inputs(seed: int = 0) -> dict:
    seeds = jax.random.split(jax.random.key(seed), 5)
    return {
        "queries": draw_queries(jax.random.fold_in(seeds[4], 71), 0),
        "keys": draw_keys(jax.random.fold_in(seeds[4], 71), 0),
        "values": centred(seeds[2], (TOKENS, D), 1.0, 6.0, ((0, 256),), jnp.float32),
        "cotangent": centred(seeds[3], (TOKENS, D), 1.0, 6.0, ((0, 256),), jnp.float32),
    }


LOG_TWO = math.log(2.0)
HIGHEST_PRECISION = lax.Precision.HIGHEST

def halve_rows(matrix):
    paired = matrix.reshape(matrix.shape[0] // 2, 2, matrix.shape[1])
    return 0.5 * (paired[:, 0] + paired[:, 1])

def reference(queries, keys, values, cotangent):
    total_tokens = queries.shape[0]
    features = queries.shape[1]
    head_dim = features // HEADS
    blocks = total_tokens // BLOCK
    depth = blocks.bit_length() - 1
    score_scale = 1.0 / math.sqrt(head_dim)
    paired_rows = jnp.concatenate([keys, values], axis=1)
    coarse = [paired_rows]
    for height in range(1, depth):
        coarse.append(halve_rows(coarse[-1]))
    offsets = jnp.array([0.0] + [height * LOG_TWO for height in range(depth)], queries.dtype)
    pending_start = tuple((jnp.zeros_like(matrix) for matrix in coarse))

    def advance(pending, number):
        first_row = (number * BLOCK).astype(jnp.int32)
        query_block = lax.dynamic_slice_in_dim(queries, first_row, BLOCK, 0).reshape(BLOCK, HEADS, head_dim)
        grad_block = lax.dynamic_slice_in_dim(cotangent, first_row, BLOCK, 0).reshape(BLOCK, HEADS, head_dim)
        key_sets = [lax.dynamic_slice_in_dim(paired_rows, first_row, BLOCK, 0)]
        starts = []
        for height in range(depth):
            segment = number // 2 ** height
            sibling = segment + 1 - 2 * (segment % 2)
            sibling_row = (sibling * BLOCK).astype(jnp.int32)
            starts.append(sibling_row)
            key_sets.append(lax.dynamic_slice_in_dim(coarse[height], sibling_row, BLOCK, 0))
        stacked = jnp.stack(key_sets).reshape(depth + 1, BLOCK, 2, HEADS, head_dim)
        key_part = stacked[:, :, 0]
        value_part = stacked[:, :, 1]
        scores = jnp.einsum('qhd,jkhd->hqjk', query_block, key_part, precision=HIGHEST_PRECISION) * score_scale
        scores = scores + offsets[None, None, :, None]
        highest = lax.optimization_barrier(jnp.max(scores, axis=(2, 3), keepdims=True))
        exponent = jnp.exp(scores - highest)
        weights = exponent / lax.optimization_barrier(jnp.sum(exponent, axis=(2, 3), keepdims=True))
        attended = jnp.einsum('hqjk,jkhd->qhd', weights, value_part, precision=HIGHEST_PRECISION)
        row_dot = lax.optimization_barrier(jnp.sum(attended * grad_block, axis=2))
        prob_grad = jnp.einsum('qhd,jkhd->hqjk', grad_block, value_part, precision=HIGHEST_PRECISION)
        score_grad = weights * (prob_grad - row_dot.T[:, :, None, None])
        query_grad = jnp.einsum('hqjk,jkhd->qhd', score_grad, key_part, precision=HIGHEST_PRECISION) * score_scale
        key_grad = jnp.einsum('hqjk,qhd->jkhd', score_grad, query_block, precision=HIGHEST_PRECISION) * score_scale
        value_grad = jnp.einsum('hqjk,qhd->jkhd', weights, grad_block, precision=HIGHEST_PRECISION)
        pair_grad = jnp.stack([key_grad, value_grad], axis=2).reshape(depth + 1, BLOCK, 2 * features)
        updated = []
        for height in range(depth):
            present = lax.dynamic_slice_in_dim(pending[height], starts[height], BLOCK, 0)
            updated.append(lax.dynamic_update_slice_in_dim(pending[height], present + pair_grad[height + 1], starts[height], 0))
        return (tuple(updated), (attended.reshape(BLOCK, features), query_grad.reshape(BLOCK, features), pair_grad[0]))
    pending, (attended_rows, query_rows, own_rows) = lax.scan(advance, pending_start, jnp.arange(blocks, dtype=jnp.int32))
    token_grad = own_rows.reshape(total_tokens, 2 * features)
    for height in range(depth):
        token_grad = token_grad + jnp.repeat(pending[height] / 2 ** height, 2 ** height, axis=0)
    attended = attended_rows.reshape(total_tokens, features)
    query_grad = query_rows.reshape(total_tokens, features)
    return (attended, query_grad, token_grad[:, :features], token_grad[:, features:])
```

```python
import functools
import math

import jax
import jax.numpy as jnp
from jax import lax
from jax.experimental import pallas as pl
from jax.experimental.pallas import tpu as pltpu
from jax.sharding import PartitionSpec as P

MESH = pl.DeviceIdType.MESH
F32 = jnp.float32
BF16 = jnp.bfloat16
HEADS = 12
HD = 64
B = 128
LOG_TWO = math.log(2.0)
NT = (((1,), (1,)), ((), ()))

OWN_A, OWN_B, C1_A, C1_B, C2_A, SIB_A, C2_O, SIB_B, SETS = 0, 8, 12, 16, 18, 20, 25, 26, 31


def dot(a, b, dims=(((1,), (0,)), ((), ()))):
    return lax.dot_general(a, b, dims, preferred_element_type=F32)


def split(v):
    hi = v.astype(BF16)
    return hi, (v - hi.astype(F32)).astype(BF16)


def rows(start, count):
    return pl.ds(pl.multiple_of(start, 8), count)


def kernel(
    q_ref, k_ref, v_ref, g_ref,
    oa_ref, oq_ref, ok_ref, ov_ref,
    kvs, qgs, kvr, qgr, c2o, cs3, cs4, cs5, cs6, cs7, sib,
    hl, hlt, xs, xt, sd, pdh, pdl, ga, xr, gs, gr, u3, u4, u5, u6, u7, rqa, fqa, fkv,
    kv_s, kv_r, qg_s, qg_r, cx_s, cx_r, sb_s, sb_r, gx_s, gx_r, gs_s, gs_r, rq_s, rq_r, rk_s, rk_r,
):
    hi_id, lo_id = lax.axis_index("seqhi"), lax.axis_index("seqlo")
    x, k = lax.div(hi_id, 2), lax.rem(hi_id, 2)
    y, z = lax.div(lo_id, 8), lax.rem(lo_id, 8)
    cw = lax.rem(z, 2)
    t = lax.div(z, 2)
    quad = lax.div(z, 4)
    p = x * 8 + cw * 4 + y
    other = (x * 2 + 1 - k, lo_id)
    here = cw == k

    def subtree_device(pp):
        xx, rest = lax.div(pp, 8), lax.rem(pp, 8)
        return (xx * 2 + k, lax.rem(rest, 4) * 8 + 2 * t + lax.div(rest, 4))

    barrier = pltpu.get_barrier_semaphore()

    def greet(dev):
        pl.semaphore_signal(barrier, inc=1, device_id=dev, device_id_type=MESH)

    def greet_ring(i, _):
        @pl.when(jnp.logical_not(here & (i == z)))
        def _():
            greet((x * 2 + cw, y * 8 + i))
        wk, wz = lax.rem(i, 2), 2 * lax.div(i, 2) + k

        @pl.when(jnp.logical_not((wk == k) & (wz == z)))
        def _():
            greet((x * 2 + wk, y * 8 + wz))
        return 0

    lax.fori_loop(0, 8, greet_ring, 0)
    greet(other)

    def greet_sub(i, _):
        greet(subtree_device(lax.rem(p + i, 32)))
        return 0

    lax.fori_loop(1, 32, greet_sub, 0)

    low = lax.broadcasted_iota(jnp.int32, (B, B), 1) < HD

    def pack(a_ref, b_ref, dst, scale):
        for pair in range(HEADS // 2):
            cols = slice(pair * B, (pair + 1) * B)
            a, b = a_ref[:, cols], b_ref[:, cols]
            if scale != 1.0:
                a = a * scale
            dst[2 * pair] = jnp.where(low, a, pltpu.roll(b, HD, 1))
            dst[2 * pair + 1] = jnp.where(low, pltpu.roll(a, HD, 1), b)

    pack(k_ref, v_ref, kvs, 1.0)
    pl.semaphore_wait(barrier, 48 - 2 * (1 - lax.rem(cw + k, 2)))

    def send_out(src, dst, ssem, rsem):
        def step(i, _):
            u = lax.rem(i + t, 4)
            wz = 2 * u + k
            for j in range(3):
                h = 3 * u + j
                wk = (0, quad, 1)[j]
                slot = z if j != 1 else 8 + lax.rem(z, 4)
                me = (wz == z) & (wk == k)

                @pl.when(me)
                def _():
                    pltpu.make_async_copy(src.at[h], dst.at[rows(slot * B, B)], rsem.at[slot]).start()

                @pl.when(jnp.logical_not(me))
                def _():
                    pltpu.make_async_remote_copy(
                        src.at[h], dst.at[rows(slot * B, B)], ssem.at[h], rsem.at[slot],
                        device_id=(x * 2 + wk, y * 8 + wz), device_id_type=MESH,
                    ).start()
            return 0

        lax.fori_loop(0, 4, step, 0)

    def sent_out(src, ssem):
        def step(u, _):
            wz = 2 * u + k
            for j in range(3):
                h = 3 * u + j
                wk = (0, quad, 1)[j]

                @pl.when(jnp.logical_not((wz == z) & (wk == k)))
                def _():
                    pltpu.make_async_copy(src.at[h], src.at[h], ssem.at[h]).wait()
            return 0

        lax.fori_loop(0, 4, step, 0)

    def landed(dst, rsem, slot):
        part = dst.at[rows(slot * B, B)]
        pltpu.make_async_copy(part, part, rsem.at[slot]).wait()

    def send_back(src, dst, ssem, rsem, slot, job):
        if job == 0:
            oz, h = slot, 3 * t + 2 * k
        else:
            oz, h = 4 * k + slot - OWN_B, 3 * t + 1
        me = here & (oz == z)
        part = src.at[rows(slot * B, B)]

        @pl.when(me)
        def _():
            pltpu.make_async_copy(part, dst.at[h], rsem.at[h]).start()

        @pl.when(jnp.logical_not(me))
        def _():
            pltpu.make_async_remote_copy(
                part, dst.at[h], ssem.at[slot], rsem.at[h],
                device_id=(x * 2 + cw, y * 8 + oz), device_id_type=MESH,
            ).start()

    def sent_back(src, ssem, slot, job):
        oz = slot if job == 0 else 4 * k + slot - OWN_B

        @pl.when(jnp.logical_not(here & (oz == z)))
        def _():
            part = src.at[rows(slot * B, B)]
            pltpu.make_async_copy(part, part, ssem.at[slot]).wait()

    def send_subtrees(m, src_part, dst, ssem, rsem):
        size = 2**m
        n = B // size
        group = lax.div(p, size)
        base = (group + 1 - 2 * lax.rem(group, 2)) * size
        mine = lax.rem(p, size) * n

        def step(i, _):
            j = lax.rem(i + p, size)
            pltpu.make_async_remote_copy(
                src_part(j, n), dst.at[m, :, rows(mine, n), :], ssem.at[m], rsem.at[m],
                device_id=subtree_device(base + j), device_id_type=MESH,
            ).start()
            return 0

        lax.fori_loop(0, size, step, 0)

    def wait_all(ref, sem):
        pltpu.make_async_copy(ref, ref, sem).wait()

    send_out(kvs, kvr, kv_s, kv_r)
    pack(q_ref, g_ref, qgs, 0.125)
    ga[...] = jnp.zeros_like(ga)
    sent_out(kvs, kv_s)
    send_out(qgs, qgr, qg_s, qg_r)

    def put(index, v):
        h, l = split(v)
        hl[index, :, 0:B] = h
        hl[index, :, B : 2 * B] = l
        th, tl = split(v.T)
        hlt[index, 0:B, :] = th
        hlt[index, B : 2 * B, :] = tl

    def halve(ref, start, n):
        return 0.5 * (ref[pl.ds(start, n, stride=2), :] + ref[pl.ds(start + 1, n, stride=2), :])

    for s in range(OWN_B, 12):
        landed(kvr, kv_r, s)
    for i in range(2):
        kvr[(C1_B + i) * B : (C1_B + i + 1) * B] = halve(kvr, (OWN_B + 2 * i) * B, B)
    kvr[30 * B : 31 * B] = halve(kvr, C1_B * B, B)
    c2_mine = kvr.at[pl.ds(30 * B, B)]
    cx = pltpu.make_async_remote_copy(c2_mine, c2o, cx_s, cx_r, device_id=other, device_id_type=MESH)
    cx.start()
    for s in range(8):
        landed(kvr, kv_r, s)
    for i in range(4):
        kvr[(C1_A + i) * B : (C1_A + i + 1) * B] = halve(kvr, (OWN_A + 2 * i) * B, B)
    for i in range(2):
        kvr[(C2_A + i) * B : (C2_A + i + 1) * B] = halve(kvr, (C1_A + 2 * i) * B, B)
    cs3[0] = halve(kvr, C2_A * B, B)
    cs3[1, rows(64 * k, 64), :] = halve(kvr, 30 * B, 64)
    cx.wait_recv()
    cs3[1, rows(64 * (1 - k), 64), :] = halve(c2o, 0, 64)
    levels = (cs3, cs4, cs5, cs6, cs7)
    for m in range(5):
        if m:
            for job in range(2):
                levels[m][job] = halve(levels[m - 1].at[job], 0, B >> m)
        send_subtrees(m, lambda j, n: levels[m], sib, sb_s, sb_r)

    def put_step(i, _):
        put(i, kvr[rows(i * B, B), :])
        return 0

    lax.fori_loop(0, 20, put_step, 0)
    put(C2_O, c2o[...])
    for m in range(5):
        wait_all(sib.at[m], sb_r.at[m])

    def put_sib(m, _):
        put(SIB_A + m, sib[m, 0])
        put(SIB_B + m, sib[m, 1])
        return 0

    lax.fori_loop(0, 5, put_sib, 0)

    def load_set(position, index):
        part = slice(position * B, (position + 1) * B)
        h = hl[index, :, 0:B]
        xs[part, 0:B] = h
        xs[part, B : 2 * B] = hl[index, :, B : 2 * B]
        xs[part, 2 * B : 3 * B] = h
        xt[:, part] = hlt[index]

    def flip(i):
        return i + 1 - 2 * lax.rem(i, 2)

    def run_task(b, job):
        own, c1, sibs = ((OWN_A, C1_A, SIB_A), (OWN_B, C1_B, SIB_B))[job]
        slot = own + b
        indices = [slot, own + flip(b), c1 + flip(lax.div(b, 2))]
        indices.append(C2_A + flip(lax.div(b, 4)) if job == 0 else C2_O)
        indices += [sibs + m for m in range(5)]
        for position in range(4):
            load_set(position, indices[position])
        landed(qgr, qg_r, slot)
        qh, ql = split(qgr[rows(slot * B, B), :])
        zero = jnp.zeros_like(qh)
        wide = jnp.concatenate(
            [
                jnp.concatenate([jnp.where(low, qh, zero), jnp.where(low, ql, zero)], axis=1),
                jnp.concatenate([jnp.where(low, zero, qh), jnp.where(low, zero, ql)], axis=1),
            ],
            axis=0,
        )
        w = jnp.concatenate([wide[:, 0:B], wide], axis=1)
        sd[...] = dot(xs[...], w, NT)
        top = jnp.full((8, B), -jnp.inf, F32)
        offsets = [max(i - 1, 0) * LOG_TWO for i in range(9)]
        for i in range(9):
            s = sd[i * B : (i + 1) * B, 0:B]
            top = jnp.maximum(top, jnp.max(s.reshape(16, 8, B), axis=0) + offsets[i])
        top = jnp.max(top, axis=0, keepdims=True)
        total = jnp.zeros((8, B), F32)
        along = jnp.zeros((8, B), F32)
        for i in range(9):
            part = slice(i * B, (i + 1) * B)
            e = jnp.exp(sd[part, 0:B] - (top - offsets[i]))
            sd[part, 0:B] = e
            total = total + jnp.sum(e.reshape(16, 8, B), axis=0)
            along = along + jnp.sum((e * sd[part, B : 2 * B]).reshape(16, 8, B), axis=0)
        norm = 1.0 / jnp.sum(total, axis=0, keepdims=True)
        row_dot = jnp.sum(along, axis=0, keepdims=True) * norm
        for i in range(9):
            part = slice(i * B, (i + 1) * B)
            prob = sd[part, 0:B] * norm
            ds = prob * (sd[part, B : 2 * B] - row_dot)
            pdh[part, 0:B], pdl[part, 0:B] = split(ds)
            pdh[part, B : 2 * B], pdl[part, B : 2 * B] = split(prob)
        high = pdh[...]
        out = dot(xt[...], high)
        out = out[0:B] + out[B : 2 * B] + dot(xt[0:B], pdl[...])
        both = jnp.concatenate([out[0:HD, 0:B] * 0.125, out[HD : 2 * HD, B : 2 * B]], axis=0)
        rqa[rows(slot * B, B), :] = both.T
        send_back(rqa, fqa, rq_s, rq_r, slot, job)
        sd[...] = dot(high, wide)
        grads = dot(pdl[...], wide[:, 0:B])
        for i in range(9):
            part = slice(i * B, (i + 1) * B)
            dst = rows(indices[i] * B, B)
            ga[dst, :] = ga[dst, :] + (sd[part, 0:B] + sd[part, B : 2 * B] + grads[part])

    def run_job(job, count):
        for m in range(5):
            load_set(4 + m, (SIB_A, SIB_B)[job] + m)

        def step(b, _):
            run_task(b, job)
            return 0

        lax.fori_loop(0, count, step, 0)

    run_job(1, 4)
    gx_src = ga.at[pl.ds(C2_O * B, 6 * B)]
    gx = pltpu.make_async_remote_copy(gx_src, xr, gx_s, gx_r, device_id=other, device_id_type=MESH)
    gx.start()
    run_job(0, 8)
    gx.wait()
    for m in range(5):
        gs[m, 0] = ga[(SIB_A + m) * B : (SIB_A + m + 1) * B]
        gs[m, 1] = ga[(SIB_B + m) * B : (SIB_B + m + 1) * B] + xr[(1 + m) * B : (2 + m) * B]
        send_subtrees(m, lambda j, n: gs.at[m, :, rows(j * n, n), :], gr, gs_s, gs_r)

    ups = (u3, u4, u5, u6, u7)
    for m in (4, 3, 2, 1, 0):
        wait_all(gr.at[m], gs_r.at[m])
        n = B >> m
        for job in range(2):
            acc = gr[m, job, 0:n]
            for j in range(1, 2**m):
                acc = acc + gr[m, job, j * n : (j + 1) * n]
            ups[m][job] = acc

    def spread(src, dst, start, n):
        half = 0.5 * src
        for odd in range(2):
            at = pl.ds(start + odd, n, stride=2)
            dst[at, :] = dst[at, :] + half

    for m in (4, 3, 2, 1):
        for job in range(2):
            spread(ups[m][job], ups[m - 1].at[job], 0, B >> m)
    spread(u3[0], ga, C2_A * B, B)
    for i in range(2):
        spread(ga[(C2_A + i) * B : (C2_A + i + 1) * B], ga, (C1_A + 2 * i) * B, B)
    for i in range(4):
        spread(ga[(C1_A + i) * B : (C1_A + i + 1) * B], ga, (OWN_A + 2 * i) * B, B)
    spread(u3[1, rows(64 * k, 64), :], xr, 0, 64)
    spread(xr[0:B], ga, C1_B * B, B)
    for i in range(2):
        spread(ga[(C1_B + i) * B : (C1_B + i + 1) * B], ga, (OWN_B + 2 * i) * B, B)

    def back_a(i, _):
        send_back(ga, fkv, rk_s, rk_r, i, 0)
        return 0

    def back_b(i, _):
        send_back(ga, fkv, rk_s, rk_r, i, 1)
        return 0

    lax.fori_loop(0, 8, back_a, 0)
    lax.fori_loop(8, 12, back_b, 0)

    def unpack(src, rsem, first_ref, last_ref):
        for pair in range(HEADS // 2):
            for h in (2 * pair, 2 * pair + 1):
                pltpu.make_async_copy(src.at[h], src.at[h], rsem.at[h]).wait()
            even, odd = src[2 * pair], src[2 * pair + 1]
            cols = slice(pair * B, (pair + 1) * B)
            first_ref[:, cols] = jnp.where(low, even, pltpu.roll(odd, HD, 1))
            last_ref[:, cols] = jnp.where(low, pltpu.roll(even, HD, 1), odd)

    unpack(fqa, rq_r, oq_ref, oa_ref)
    unpack(fkv, rk_r, ok_ref, ov_ref)

    sent_out(qgs, qg_s)
    cx.wait_send()
    for m in range(5):
        wait_all(sib.at[m], sb_s.at[m])
        wait_all(gr.at[m], gs_s.at[m])

    def done_a(i, _):
        sent_back(rqa, rq_s, i, 0)
        sent_back(ga, rk_s, i, 0)
        return 0

    def done_b(i, _):
        sent_back(rqa, rq_s, i, 1)
        sent_back(ga, rk_s, i, 1)
        return 0

    lax.fori_loop(0, 8, done_a, 0)
    lax.fori_loop(8, 12, done_b, 0)


def on_device(queries, keys, values, cotangent):
    shape = jax.ShapeDtypeStruct(queries.shape, F32)
    vm = pl.BlockSpec(memory_space=pltpu.VMEM)
    dma = pltpu.SemaphoreType.DMA
    scratch = [
        pltpu.VMEM((12, B, B), F32),
        pltpu.VMEM((12, B, B), F32),
        pltpu.VMEM((SETS * B, B), F32),
        pltpu.VMEM((12 * B, B), F32),
        pltpu.VMEM((B, B), F32),
    ]
    scratch += [pltpu.VMEM((2, B >> m, B), F32) for m in range(5)]
    scratch += [
        pltpu.VMEM((5, 2, B, B), F32),
        pltpu.VMEM((SETS, B, 2 * B), BF16),
        pltpu.VMEM((SETS, 2 * B, B), BF16),
        pltpu.VMEM((9 * B, 3 * B), BF16),
        pltpu.VMEM((2 * B, 9 * B), BF16),
        pltpu.VMEM((9 * B, 2 * B), F32),
        pltpu.VMEM((9 * B, 2 * B), BF16),
        pltpu.VMEM((9 * B, 2 * B), BF16),
        pltpu.VMEM((SETS * B, B), F32),
        pltpu.VMEM((6 * B, B), F32),
        pltpu.VMEM((5, 2, B, B), F32),
        pltpu.VMEM((5, 2, B, B), F32),
    ]
    scratch += [pltpu.VMEM((2, B >> m, B), F32) for m in range(5)]
    scratch += [
        pltpu.VMEM((12 * B, B), F32),
        pltpu.VMEM((12, B, B), F32),
        pltpu.VMEM((12, B, B), F32),
    ]
    scratch += [dma((12,))] * 4 + [dma] * 2 + [dma((5,))] * 2 + [dma] * 2 + [dma((5,))] * 2 + [dma((12,))] * 4
    return pl.pallas_call(
        kernel,
        out_shape=[shape] * 4,
        in_specs=[vm] * 4,
        out_specs=[vm] * 4,
        scratch_shapes=scratch,
        compiler_params=pltpu.CompilerParams(
            collective_id=0, has_side_effects=True, vmem_limit_bytes=56 * 2**20
        ),
    )(queries, keys, values, cotangent)


def solution(mesh):
    spec = P(("seqhi", "seqlo"), None)
    return jax.shard_map(
        on_device, mesh=mesh, in_specs=(spec,) * 4, out_specs=(spec,) * 4, check_vma=False
    )
```

```python
import functools
import math

import jax
import jax.numpy as jnp
from jax import lax
from jax.experimental import pallas as pl
from jax.experimental.pallas import tpu as pltpu
from jax.sharding import PartitionSpec as P

MESH = pl.DeviceIdType.MESH
F32 = jnp.float32
BF16 = jnp.bfloat16
HEADS = 12
HD = 64
B = 128
LOG_TWO = math.log(2.0)
NT = (((1,), (1,)), ((), ()))

OWN_A, OWN_B, C1_A, C1_B, C2_A, SIB_A, C2_O, SIB_B, SETS = 0, 8, 12, 16, 18, 20, 25, 26, 31


def dot(a, b, dims=(((1,), (0,)), ((), ()))):
    return lax.dot_general(a, b, dims, preferred_element_type=F32)


def split(v):
    hi = v.astype(BF16)
    return hi, (v - hi.astype(F32)).astype(BF16)


def rows(start, count):
    return pl.ds(pl.multiple_of(start, 8), count)


def kernel(
    q_hbm, k_hbm, v_hbm, g_hbm,
    fqa, fkv, fc3,
    q_ref, k_ref, v_ref, g_ref,
    kvs, qgs, kvr, qgr, c2o, cs3, cs4, cs5, cs6, cs7, sib,
    hl, hlt, xs, xt, sd, dp, ph, plo, dh, dl, ga, xr, gs, gr, u3, u4, u5, u6, u7, rqa,
    in_s, kv_s, kv_r, qg_s, qg_r, cx_s, cx_r, sb_s, sb_r, gx_s, gx_r, gs_s, gs_r,
    rq_s, rq_r, rk_s, rk_r, rc_s, rc_r,
):
    hi_id, lo_id = lax.axis_index("seqhi"), lax.axis_index("seqlo")
    x, k = lax.div(hi_id, 2), lax.rem(hi_id, 2)
    y, z = lax.div(lo_id, 8), lax.rem(lo_id, 8)
    cw = lax.rem(z, 2)
    t = lax.div(z, 2)
    quad = lax.div(z, 4)
    p = x * 8 + cw * 4 + y
    other = (x * 2 + 1 - k, lo_id)
    here = cw == k

    def subtree_device(pp):
        xx, rest = lax.div(pp, 8), lax.rem(pp, 8)
        return (xx * 2 + k, lax.rem(rest, 4) * 8 + 2 * t + lax.div(rest, 4))

    loads = [
        pltpu.make_async_copy(src, dst, in_s.at[i])
        for i, (src, dst) in enumerate(((k_hbm, k_ref), (v_hbm, v_ref), (q_hbm, q_ref), (g_hbm, g_ref)))
    ]
    for load in loads:
        load.start()

    barrier = pltpu.get_barrier_semaphore()

    def greet(dev):
        pl.semaphore_signal(barrier, inc=1, device_id=dev, device_id_type=MESH)

    def greet_ring(i, _):
        @pl.when(jnp.logical_not(here & (i == z)))
        def _():
            greet((x * 2 + cw, y * 8 + i))
        wk, wz = lax.rem(i, 2), 2 * lax.div(i, 2) + k

        @pl.when(jnp.logical_not((wk == k) & (wz == z)))
        def _():
            greet((x * 2 + wk, y * 8 + wz))
        return 0

    lax.fori_loop(0, 8, greet_ring, 0)
    greet(other)

    def greet_sub(i, _):
        greet(subtree_device(lax.rem(p + i, 32)))
        return 0

    lax.fori_loop(1, 32, greet_sub, 0)

    low = lax.broadcasted_iota(jnp.int32, (B, B), 1) < HD

    def pack(a_ref, b_ref, dst, scale):
        for pair in range(HEADS // 2):
            cols = slice(pair * B, (pair + 1) * B)
            a, b = a_ref[:, cols], b_ref[:, cols]
            if scale != 1.0:
                a = a * scale
            dst[2 * pair] = jnp.where(low, a, pltpu.roll(b, HD, 1))
            dst[2 * pair + 1] = jnp.where(low, pltpu.roll(a, HD, 1), b)

    loads[0].wait()
    loads[1].wait()
    pack(k_ref, v_ref, kvs, 1.0)
    pl.semaphore_wait(barrier, 48 - 2 * (1 - lax.rem(cw + k, 2)))

    def send_out(src, dst, ssem, rsem, heads):
        def step(i, _):
            u = lax.rem(i + t, 4)
            wz = 2 * u + k
            for j in heads:
                h = 3 * u + j
                wk = (0, quad, 1)[j]
                slot = z if j != 1 else 8 + lax.rem(z, 4)
                me = (wz == z) & (wk == k)

                @pl.when(me)
                def _():
                    pltpu.make_async_copy(src.at[h], dst.at[rows(slot * B, B)], rsem.at[slot]).start()

                @pl.when(jnp.logical_not(me))
                def _():
                    pltpu.make_async_remote_copy(
                        src.at[h], dst.at[rows(slot * B, B)], ssem.at[h], rsem.at[slot],
                        device_id=(x * 2 + wk, y * 8 + wz), device_id_type=MESH,
                    ).start()
            return 0

        lax.fori_loop(0, 4, step, 0)

    def sent_out(src, ssem):
        def step(u, _):
            wz = 2 * u + k
            for j in range(3):
                h = 3 * u + j
                wk = (0, quad, 1)[j]

                @pl.when(jnp.logical_not((wz == z) & (wk == k)))
                def _():
                    pltpu.make_async_copy(src.at[h], src.at[h], ssem.at[h]).wait()
            return 0

        lax.fori_loop(0, 4, step, 0)

    def landed(dst, rsem, slot):
        part = dst.at[rows(slot * B, B)]
        pltpu.make_async_copy(part, part, rsem.at[slot]).wait()

    def owner(slot, job):
        if job == 0:
            return slot, 3 * t + 2 * k
        return 4 * k + slot - OWN_B, 3 * t + 1

    def send_back(part, dst, ssem, rsem, slot, job):
        oz, h = owner(slot, job)
        me = here & (oz == z)

        @pl.when(me)
        def _():
            pltpu.make_async_copy(part, dst.at[h], rsem.at[h]).start()

        @pl.when(jnp.logical_not(me))
        def _():
            pltpu.make_async_remote_copy(
                part, dst.at[h], ssem.at[slot], rsem.at[h],
                device_id=(x * 2 + cw, y * 8 + oz), device_id_type=MESH,
            ).start()

    def sent_back(part, ssem, slot, job):
        oz, _ = owner(slot, job)

        @pl.when(jnp.logical_not(here & (oz == z)))
        def _():
            pltpu.make_async_copy(part, part, ssem.at[slot]).wait()

    def block(ref, slot):
        return ref.at[rows(slot * B, B)]

    def c3_part(slot, job):
        return u3.at[job, rows(16 * owner(slot, job)[0], 16), :]

    def both_jobs(what):
        for job, (first, last) in enumerate(((0, 8), (8, 12))):
            def step(i, _, job=job):
                what(i, job)
                return 0

            lax.fori_loop(first, last, step, 0)

    def send_subtrees(m, src_part, dst, ssem, rsem):
        size = 2**m
        n = B // size
        group = lax.div(p, size)
        base = (group + 1 - 2 * lax.rem(group, 2)) * size
        mine = lax.rem(p, size) * n

        def step(i, _):
            j = lax.rem(i + p, size)
            pltpu.make_async_remote_copy(
                src_part(j, n), dst.at[m, :, rows(mine, n), :], ssem.at[m], rsem.at[m],
                device_id=subtree_device(base + j), device_id_type=MESH,
            ).start()
            return 0

        lax.fori_loop(0, size, step, 0)

    def wait_all(ref, sem):
        pltpu.make_async_copy(ref, ref, sem).wait()

    send_out(kvs, kvr, kv_s, kv_r, (1, 0, 2))
    loads[2].wait()
    loads[3].wait()
    pack(q_ref, g_ref, qgs, 0.125)
    for start, count in ((C2_A, SETS - C2_A),):
        ga[start * B : (start + count) * B] = jnp.zeros((count * B, B), F32)
    sent_out(kvs, kv_s)
    send_out(qgs, qgr, qg_s, qg_r, (1,))

    def put(index, v):
        h = v.astype(BF16)
        hf = h.astype(F32)
        l = v - hf
        kk = jnp.where(low, hf, pltpu.roll(l, HD, 1))
        vv = jnp.where(low, pltpu.roll(hf, HD, 1), l)
        hl[index, :, 0:B] = kk.astype(BF16)
        hl[index, :, B : 2 * B] = h
        hl[index, :, 2 * B : 3 * B] = vv.astype(BF16)
        hlt[index, 0:B, :] = kk.T.astype(BF16)
        hlt[index, B : 2 * B, :] = vv.T.astype(BF16)

    def halve(ref, start, n):
        return 0.5 * (ref[pl.ds(start, n, stride=2), :] + ref[pl.ds(start + 1, n, stride=2), :])

    for s in range(OWN_B, 12):
        landed(kvr, kv_r, s)
    for i in range(2):
        kvr[(C1_B + i) * B : (C1_B + i + 1) * B] = halve(kvr, (OWN_B + 2 * i) * B, B)
    kvr[30 * B : 31 * B] = halve(kvr, C1_B * B, B)
    c2_mine = kvr.at[pl.ds(30 * B, B)]
    cx = pltpu.make_async_remote_copy(c2_mine, c2o, cx_s, cx_r, device_id=other, device_id_type=MESH)
    cx.start()
    for s in range(8):
        landed(kvr, kv_r, s)
    for i in range(4):
        kvr[(C1_A + i) * B : (C1_A + i + 1) * B] = halve(kvr, (OWN_A + 2 * i) * B, B)
    for i in range(2):
        kvr[(C2_A + i) * B : (C2_A + i + 1) * B] = halve(kvr, (C1_A + 2 * i) * B, B)
    cs3[0] = halve(kvr, C2_A * B, B)
    cs3[1, rows(64 * k, 64), :] = halve(kvr, 30 * B, 64)
    cx.wait_recv()
    cs3[1, rows(64 * (1 - k), 64), :] = halve(c2o, 0, 64)
    levels = (cs3, cs4, cs5, cs6, cs7)
    for m in range(5):
        if m:
            for job in range(2):
                levels[m][job] = halve(levels[m - 1].at[job], 0, B >> m)
        send_subtrees(m, lambda j, n: levels[m], sib, sb_s, sb_r)
    send_out(qgs, qgr, qg_s, qg_r, (0, 2))

    def put_step(i, _):
        put(i, kvr[rows(i * B, B), :])
        return 0

    lax.fori_loop(0, 20, put_step, 0)
    put(C2_O, c2o[...])
    for m in range(5):
        wait_all(sib.at[m], sb_r.at[m])

    def put_sib(m, _):
        put(SIB_A + m, sib[m, 0])
        put(SIB_B + m, sib[m, 1])
        return 0

    lax.fori_loop(0, 5, put_sib, 0)

    def load_set(position, index):
        part = slice(position * B, (position + 1) * B)
        xs[part, :] = hl[index]
        xt[:, part] = hlt[index]

    def flip(i):
        return i + 1 - 2 * lax.rem(i, 2)

    low2 = lax.broadcasted_iota(jnp.int32, (2 * B, B), 1) < HD

    def run_pair(b, job):
        own, c1 = ((OWN_A, C1_A), (OWN_B, C1_B))[job]
        first = own + 2 * b
        side = c1 + flip(b)
        far = C2_A + flip(lax.div(b, 2)) if job == 0 else C2_O
        load_set(0, first)
        load_set(1, first + 1)
        load_set(2, side)
        load_set(3, far)
        landed(qgr, qg_r, first)
        landed(qgr, qg_r, first + 1)
        qg = qgr[rows(first * B, 2 * B), :]
        zero = jnp.zeros_like(qg)

        def halves(v):
            h = v.astype(BF16).astype(F32)
            return h, v - h

        h, l = halves(jnp.where(low2, qg * math.log2(math.e), qg))
        turned = pltpu.roll(h, HD, 1)
        rq = jnp.concatenate([jnp.where(low2, h, turned), jnp.where(low2, l, zero)], axis=1).astype(BF16)
        rg = jnp.concatenate([jnp.where(low2, zero, l), jnp.where(low2, turned, h)], axis=1).astype(BF16)
        sd[...] = dot(xs[:, 0 : 2 * B], rq, NT)
        dp[...] = dot(xs[:, B : 3 * B], rg, NT)
        top = jnp.full((8, 2 * B), -jnp.inf, F32)
        offsets = [float(max(i - 1, 0)) for i in range(9)]
        for i in range(9):
            s = sd[i * B : (i + 1) * B]
            top = jnp.maximum(top, jnp.max(s.reshape(16, 8, 2 * B), axis=0) + offsets[i])
        top = jnp.max(top, axis=0, keepdims=True)
        total = jnp.zeros((8, 2 * B), F32)
        along = jnp.zeros((8, 2 * B), F32)
        for i in range(9):
            part = slice(i * B, (i + 1) * B)
            e = jnp.exp2(sd[part] - (top - offsets[i]))
            sd[part] = e
            total = total + jnp.sum(e.reshape(16, 8, 2 * B), axis=0)
            along = along + jnp.sum((e * dp[part]).reshape(16, 8, 2 * B), axis=0)
        norm = 1.0 / jnp.sum(total, axis=0, keepdims=True)
        row_dot = jnp.sum(along, axis=0, keepdims=True) * norm
        for i in range(9):
            part = slice(i * B, (i + 1) * B)
            prob = sd[part] * norm
            ph[part], plo[part] = split(prob)
            dh[part], dl[part] = split(prob * (dp[part] - row_dot))

        dq = dot(xt[0:B], dh[...])
        dq = dq[0:HD] + dq[HD:B] + dot(xt[0:HD], dl[...])
        at = dot(xt[B : 2 * B], ph[...])
        at = at[0:HD] + at[HD:B] + dot(xt[B : B + HD], plo[...])
        rqa[rows(first * B, 2 * B), :] = jnp.concatenate([dq * 0.125, at], axis=0).T
        for s in range(2):
            send_back(block(rqa, first + s), fqa, rq_s, rq_r, first + s, job)

        h, l = halves(qg)
        rk = jnp.concatenate([jnp.where(low2, h, zero), jnp.where(low2, l, zero)], axis=1).astype(BF16)
        rv = jnp.concatenate([jnp.where(low2, zero, h), jnp.where(low2, zero, l)], axis=1).astype(BF16)
        high = dot(dh[...], rk) + dot(ph[...], rv)
        grads = high[:, 0:B] + high[:, B : 2 * B] + (dot(dl[...], rk[:, 0:B]) + dot(plo[...], rv[:, 0:B]))
        ga[rows(first * B, 2 * B), :] = grads[0 : 2 * B]
        ga[rows(side * B, B), :] = grads[2 * B : 3 * B]
        ga[rows(far * B, B), :] = ga[rows(far * B, B), :] + grads[3 * B : 4 * B]
        top_sets = slice((SIB_A, SIB_B)[job] * B, ((SIB_A, SIB_B)[job] + 5) * B)
        ga[top_sets] = ga[top_sets] + grads[4 * B :]

    def run_job(job, count):
        for m in range(5):
            load_set(4 + m, (SIB_A, SIB_B)[job] + m)

        def step(i, _):
            run_pair(i if job else lax.rem(t + 4 - i, 4), job)
            return 0

        lax.fori_loop(0, count, step, 0)

    def spread(src, dst, start, n):
        half = 0.5 * src
        for odd in range(2):
            at = pl.ds(start + odd, n, stride=2)
            dst[at, :] = dst[at, :] + half

    run_job(1, 2)
    gx_src = ga.at[pl.ds(C2_O * B, 6 * B)]
    gx = pltpu.make_async_remote_copy(gx_src, xr, gx_s, gx_r, device_id=other, device_id_type=MESH)
    gx.start()
    run_job(0, 4)
    gx.wait()
    for m in range(5):
        gs[m, 0] = ga[(SIB_A + m) * B : (SIB_A + m + 1) * B]
        gs[m, 1] = ga[(SIB_B + m) * B : (SIB_B + m + 1) * B] + xr[(1 + m) * B : (2 + m) * B]
        send_subtrees(m, lambda j, n: gs.at[m, :, rows(j * n, n), :], gr, gs_s, gs_r)

    for i in range(2):
        spread(ga[(C2_A + i) * B : (C2_A + i + 1) * B], ga, (C1_A + 2 * i) * B, B)
    for i in range(4):
        spread(ga[(C1_A + i) * B : (C1_A + i + 1) * B], ga, (OWN_A + 2 * i) * B, B)
    spread(xr[0:B], ga, C1_B * B, B)
    for i in range(2):
        spread(ga[(C1_B + i) * B : (C1_B + i + 1) * B], ga, (OWN_B + 2 * i) * B, B)
    both_jobs(lambda i, job: send_back(block(ga, i), fkv, rk_s, rk_r, i, job))

    ups = (u3, u4, u5, u6, u7)
    for m in (4, 3, 2, 1, 0):
        wait_all(gr.at[m], gs_r.at[m])
        n = B >> m
        for job in range(2):
            acc = gr[m, job, 0:n]
            for j in range(1, 2**m):
                acc = acc + gr[m, job, j * n : (j + 1) * n]
            ups[m][job] = acc
    for m in (4, 3, 2, 1):
        for job in range(2):
            spread(ups[m][job], ups[m - 1].at[job], 0, B >> m)
    both_jobs(lambda i, job: send_back(c3_part(i, job), fc3, rc_s, rc_r, i, job))

    sent_out(qgs, qg_s)
    cx.wait_send()
    for m in range(5):
        wait_all(sib.at[m], sb_s.at[m])
        wait_all(gr.at[m], gs_s.at[m])

    def finish(i, job):
        sent_back(block(rqa, i), rq_s, i, job)
        sent_back(block(ga, i), rk_s, i, job)
        sent_back(c3_part(i, job), rc_s, i, job)
        for dst, sem in ((fqa, rq_r), (fkv, rk_r), (fc3, rc_r)):
            pltpu.make_async_copy(dst.at[i], dst.at[i], sem.at[i]).wait()

    both_jobs(finish)


def unpack(qa, kv, c3, oa, oq, ok, ov):
    low = lax.broadcasted_iota(jnp.int32, (B, B), 1) < HD

    def pair(even, odd, first, last):
        first[...] = jnp.where(low, even, pltpu.roll(odd, HD, 1))
        last[...] = jnp.where(low, pltpu.roll(even, HD, 1), odd)

    def whole(h):
        above = jnp.broadcast_to(c3[h][:, None, :] * 0.125, (16, 8, B)).reshape(B, B)
        return kv[h] + above

    pair(qa[0], qa[1], oq, oa)
    pair(whole(0), whole(1), ok, ov)


def on_device(queries, keys, values, cotangent):
    hbm = pl.BlockSpec(memory_space=pl.ANY)
    dma = pltpu.SemaphoreType.DMA
    scratch = [pltpu.VMEM(queries.shape, F32)] * 4
    scratch += [
        pltpu.VMEM((12, B, B), F32),
        pltpu.VMEM((12, B, B), F32),
        pltpu.VMEM((SETS * B, B), F32),
        pltpu.VMEM((12 * B, B), F32),
        pltpu.VMEM((B, B), F32),
    ]
    scratch += [pltpu.VMEM((2, B >> m, B), F32) for m in range(5)]
    scratch += [
        pltpu.VMEM((5, 2, B, B), F32),
        pltpu.VMEM((SETS, B, 3 * B), BF16),
        pltpu.VMEM((SETS, 2 * B, B), BF16),
        pltpu.VMEM((9 * B, 3 * B), BF16),
        pltpu.VMEM((2 * B, 9 * B), BF16),
        pltpu.VMEM((9 * B, 2 * B), F32),
        pltpu.VMEM((9 * B, 2 * B), F32),
    ]
    scratch += [pltpu.VMEM((9 * B, 2 * B), BF16)] * 4
    scratch += [
        pltpu.VMEM((SETS * B, B), F32),
        pltpu.VMEM((6 * B, B), F32),
        pltpu.VMEM((5, 2, B, B), F32),
        pltpu.VMEM((5, 2, B, B), F32),
    ]
    scratch += [pltpu.VMEM((2, B >> m, B), F32) for m in range(5)]
    scratch += [
        pltpu.VMEM((12 * B, B), F32),
    ]
    scratch += [dma((4,))] + [dma((12,))] * 4 + [dma] * 2 + [dma((5,))] * 2 + [dma] * 2 + [dma((5,))] * 2
    scratch += [dma((12,))] * 6
    packed = pl.pallas_call(
        kernel,
        out_shape=[jax.ShapeDtypeStruct((12, n, B), F32) for n in (B, B, 16)],
        in_specs=[hbm] * 4,
        out_specs=[hbm] * 3,
        scratch_shapes=scratch,
        compiler_params=pltpu.CompilerParams(
            collective_id=0, has_side_effects=True, vmem_limit_bytes=56 * 2**20
        ),
    )(queries, keys, values, cotangent)
    return pl.pallas_call(
        unpack,
        grid=(HEADS // 2,),
        out_shape=[jax.ShapeDtypeStruct(queries.shape, F32)] * 4,
        in_specs=[pl.BlockSpec((2, n, B), lambda i: (i, 0, 0)) for n in (B, B, 16)],
        out_specs=[pl.BlockSpec((B, B), lambda i: (0, i))] * 4,
    )(*packed)


def solution(mesh):
    spec = P(("seqhi", "seqlo"), None)
    return jax.shard_map(
        on_device, mesh=mesh, in_specs=(spec,) * 4, out_specs=(spec,) * 4, check_vma=False
    )
```

```python
import functools
import math

import jax
import jax.numpy as jnp
from jax import lax
from jax.experimental import pallas as pl
from jax.experimental.pallas import tpu as pltpu
from jax.sharding import PartitionSpec as P

MESH = pl.DeviceIdType.MESH
F32 = jnp.float32
BF16 = jnp.bfloat16
HEADS = 12
HD = 64
B = 128
LOG_TWO = math.log(2.0)
NT = (((1,), (1,)), ((), ()))

OWN_A, OWN_B, C1_A, C1_B, C2_A, SIB_A, C2_O, SIB_B, SETS = 0, 8, 12, 16, 18, 20, 25, 26, 31


def dot(a, b, dims=(((1,), (0,)), ((), ()))):
    return lax.dot_general(a, b, dims, preferred_element_type=F32)


def split(v):
    hi = v.astype(BF16)
    return hi, (v - hi.astype(F32)).astype(BF16)


def rows(start, count):
    return pl.ds(pl.multiple_of(start, 8), count)


def kernel(
    q_hbm, k_hbm, v_hbm, g_hbm,
    fqa, fkv, fc3,
    q_ref, k_ref, v_ref, g_ref,
    kvs, qgs, kvr, qgr, c2o, cs3, cs4, cs5, cs6, cs7, sib,
    hl, hlt, xs, xt, sd, dp, ph, plo, dh, dl, ga, xr, gs, gr, u3, u4, u5, u6, u7, rqa,
    in_s, kv_s, kv_r, qg_s, qg_r, cx_s, cx_r, sb_s, sb_r, gx_s, gx_r, gs_s, gs_r,
    rq_s, rq_r, rk_s, rk_r, rc_s, rc_r,
):
    hi_id, lo_id = lax.axis_index("seqhi"), lax.axis_index("seqlo")
    x, k = lax.div(hi_id, 2), lax.rem(hi_id, 2)
    y, z = lax.div(lo_id, 8), lax.rem(lo_id, 8)
    t = lax.div(z, 2)
    cw = lax.rem(z, 2)
    quad = lax.div(z, 4)
    p = (x * 8 + k * 4 + y, x * 8 + cw * 4 + y)
    other = (x * 2 + 1 - k, lo_id)

    def subtree_device(pp, job):
        xx, rest = lax.div(pp, 8), lax.rem(pp, 8)
        cc, yy = lax.div(rest, 4), lax.rem(rest, 4)
        if job == 0:
            return (xx * 2 + cc, yy * 8 + z)
        return (xx * 2 + k, yy * 8 + 2 * t + cc)

    def worker(u, j, shared):
        if shared:
            return quad, 2 * u + k
        return k, 2 * u + lax.div(j, 2)

    def owner(slot, job):
        if job == 0:
            return k, slot, 3 * t + 2 * cw
        return cw, 4 * k + slot - OWN_B, 3 * t + 1

    loads = [
        pltpu.make_async_copy(src, dst, in_s.at[i])
        for i, (src, dst) in enumerate(((k_hbm, k_ref), (v_hbm, v_ref), (q_hbm, q_ref), (g_hbm, g_ref)))
    ]
    for load in loads:
        load.start()

    barrier = pltpu.get_barrier_semaphore()

    def greet(dev):
        pl.semaphore_signal(barrier, inc=1, device_id=dev, device_id_type=MESH)

    def greet_unless_me(core, zz):
        @pl.when(jnp.logical_not((core == k) & (zz == z)))
        def _():
            greet((x * 2 + core, y * 8 + zz))

    def greet_ring(i, _):
        greet_unless_me(k, i)
        return 0

    def greet_shared(i, _):
        greet_unless_me(*worker(i, 1, True))
        greet_unless_me(*owner(OWN_B + i, 1)[:2])
        return 0

    def greet_sub(i, _):
        greet(subtree_device(lax.rem(p[0] + i, 32), 0))
        return 0

    def greet_turned(i, _):
        greet(subtree_device(lax.div(i, 4) * 8 + (1 - cw) * 4 + lax.rem(i, 4), 1))
        return 0

    lax.fori_loop(0, 8, greet_ring, 0)
    lax.fori_loop(0, 4, greet_shared, 0)
    lax.fori_loop(1, 32, greet_sub, 0)
    lax.fori_loop(0, 16, greet_turned, 0)

    low = lax.broadcasted_iota(jnp.int32, (B, B), 1) < HD

    def pack(a_ref, b_ref, dst, scale):
        for pair in range(HEADS // 2):
            cols = slice(pair * B, (pair + 1) * B)
            a, b = a_ref[:, cols], b_ref[:, cols]
            if scale != 1.0:
                a = a * scale
            dst[2 * pair] = jnp.where(low, a, pltpu.roll(b, HD, 1))
            dst[2 * pair + 1] = jnp.where(low, pltpu.roll(a, HD, 1), b)

    loads[0].wait()
    loads[1].wait()
    pack(k_ref, v_ref, kvs, 1.0)
    pl.semaphore_wait(barrier, 62 - 2 * (1 - lax.rem(cw + k, 2)) * (1 - lax.rem(quad + k, 2)))

    def turn(i, n):
        return lax.rem(i + k * (n - 2 * i) + n, n)

    def send_head(src, dst, ssem, rsem, u, j, shared=False):
        h = 3 * u + j
        wk, wz = worker(u, j, shared)
        slot = 8 + lax.rem(z, 4) if shared else z
        me = (wz == z) & (wk == k)

        @pl.when(me)
        def _():
            pltpu.make_async_copy(src.at[h], dst.at[rows(slot * B, B)], rsem.at[slot]).start()

        @pl.when(jnp.logical_not(me))
        def _():
            pltpu.make_async_remote_copy(
                src.at[h], dst.at[rows(slot * B, B)], ssem.at[h], rsem.at[slot],
                device_id=(x * 2 + wk, y * 8 + wz), device_id_type=MESH,
            ).start()

    def send_shared(src, dst, ssem, rsem):
        def step(i, _):
            send_head(src, dst, ssem, rsem, lax.rem(t + turn(i, 4), 4), 1, True)
            return 0

        lax.fori_loop(0, 4, step, 0)

    def send_own(src, dst, ssem, rsem):
        def step(i, _):
            u = lax.rem(t + turn(i, 4), 4)
            for j in (0, 2):
                send_head(src, dst, ssem, rsem, u, j)
            return 0

        lax.fori_loop(0, 4, step, 0)

    def send_own_far(src, dst, ssem, rsem):
        def step(i, _):
            wz = lax.rem(z + turn(lax.rem(4 + i, 8), 8), 8)
            send_head(src, dst, ssem, rsem, lax.div(wz, 2), 2 * lax.rem(wz, 2))
            return 0

        lax.fori_loop(0, 8, step, 0)

    def sent_out(src, ssem):
        def step(u, _):
            for j in range(3):
                h = 3 * u + j
                wk, wz = worker(u, j, j == 1)

                @pl.when(jnp.logical_not((wz == z) & (wk == k)))
                def _():
                    pltpu.make_async_copy(src.at[h], src.at[h], ssem.at[h]).wait()
            return 0

        lax.fori_loop(0, 4, step, 0)

    def landed(dst, rsem, slot):
        part = dst.at[rows(slot * B, B)]
        pltpu.make_async_copy(part, part, rsem.at[slot]).wait()

    def send_back(part, dst, ssem, rsem, slot, job):
        oc, oz, h = owner(slot, job)
        me = (oc == k) & (oz == z)

        @pl.when(me)
        def _():
            pltpu.make_async_copy(part, dst.at[h], rsem.at[h]).start()

        @pl.when(jnp.logical_not(me))
        def _():
            pltpu.make_async_remote_copy(
                part, dst.at[h], ssem.at[slot], rsem.at[h],
                device_id=(x * 2 + oc, y * 8 + oz), device_id_type=MESH,
            ).start()

    def sent_back(part, ssem, slot, job):
        oc, oz, _ = owner(slot, job)

        @pl.when(jnp.logical_not((oc == k) & (oz == z)))
        def _():
            pltpu.make_async_copy(part, part, ssem.at[slot]).wait()

    def block(ref, slot):
        return ref.at[rows(slot * B, B)]

    def c3_part(slot, job):
        return u3.at[job, rows(16 * owner(slot, job)[1], 16), :]

    def both_jobs_round(what):
        def shared(i, _):
            what(8 + lax.rem(z + i, 4), 1)
            return 0

        def own(i, _):
            what(lax.rem(z + turn(lax.rem(4 + i, 8), 8), 8), 0)
            return 0

        lax.fori_loop(0, 4, shared, 0)
        lax.fori_loop(0, 8, own, 0)

    def both_jobs(what):
        for job, (first, last) in enumerate(((0, 8), (8, 12))):
            def step(i, _, job=job):
                what(i, job)
                return 0

            lax.fori_loop(first, last, step, 0)

    def send_subtrees(m, src_part, dst, ssem, rsem):
        size = 2**m
        n = B // size
        for job in range(2):
            group = lax.div(p[job], size)
            base = (group + 1 - 2 * lax.rem(group, 2)) * size
            mine = lax.rem(p[job], size) * n

            def step(i, _, job=job, base=base, mine=mine):
                j = lax.rem(i + p[job], size)
                pltpu.make_async_remote_copy(
                    src_part(job, j, n), dst.at[m, job, rows(mine, n), :], ssem.at[m], rsem.at[m],
                    device_id=subtree_device(base + j, job), device_id_type=MESH,
                ).start()
                return 0

            lax.fori_loop(0, size, step, 0)

    def wait_all(ref, sem):
        pltpu.make_async_copy(ref, ref, sem).wait()

    send_shared(kvs, kvr, kv_s, kv_r)
    send_own_far(kvs, kvr, kv_s, kv_r)
    loads[2].wait()
    loads[3].wait()
    pack(q_ref, g_ref, qgs, 0.125)
    for start, count in ((C2_A, SETS - C2_A),):
        ga[start * B : (start + count) * B] = jnp.zeros((count * B, B), F32)
    sent_out(kvs, kv_s)
    send_shared(qgs, qgr, qg_s, qg_r)

    def put(index, v):
        h = v.astype(BF16)
        hf = h.astype(F32)
        l = v - hf
        kk = jnp.where(low, hf, pltpu.roll(l, HD, 1))
        vv = jnp.where(low, pltpu.roll(hf, HD, 1), l)
        hl[index, :, 0:B] = kk.astype(BF16)
        hl[index, :, B : 2 * B] = h
        hl[index, :, 2 * B : 3 * B] = vv.astype(BF16)
        hlt[index, 0:B, :] = kk.T.astype(BF16)
        hlt[index, B : 2 * B, :] = vv.T.astype(BF16)

    def halve(ref, start, n):
        return 0.5 * (ref[pl.ds(start, n, stride=2), :] + ref[pl.ds(start + 1, n, stride=2), :])

    for s in range(OWN_B, 12):
        landed(kvr, kv_r, s)
    for i in range(2):
        kvr[(C1_B + i) * B : (C1_B + i + 1) * B] = halve(kvr, (OWN_B + 2 * i) * B, B)
    kvr[30 * B : 31 * B] = halve(kvr, C1_B * B, B)
    c2_mine = kvr.at[pl.ds(30 * B, B)]
    cx = pltpu.make_async_remote_copy(c2_mine, c2o, cx_s, cx_r, device_id=other, device_id_type=MESH)
    cx.start()
    for s in range(8):
        landed(kvr, kv_r, s)
    for i in range(4):
        kvr[(C1_A + i) * B : (C1_A + i + 1) * B] = halve(kvr, (OWN_A + 2 * i) * B, B)
    for i in range(2):
        kvr[(C2_A + i) * B : (C2_A + i + 1) * B] = halve(kvr, (C1_A + 2 * i) * B, B)
    cs3[0] = halve(kvr, C2_A * B, B)
    cs3[1, rows(64 * k, 64), :] = halve(kvr, 30 * B, 64)
    cx.wait_recv()
    cs3[1, rows(64 * (1 - k), 64), :] = halve(c2o, 0, 64)
    levels = (cs3, cs4, cs5, cs6, cs7)
    for m in range(5):
        if m:
            for job in range(2):
                levels[m][job] = halve(levels[m - 1].at[job], 0, B >> m)
        send_subtrees(m, lambda job, j, n: levels[m].at[job], sib, sb_s, sb_r)
    send_own(qgs, qgr, qg_s, qg_r)

    def put_step(i, _):
        put(i, kvr[rows(i * B, B), :])
        return 0

    lax.fori_loop(0, 20, put_step, 0)
    put(C2_O, c2o[...])
    for m in range(5):
        wait_all(sib.at[m], sb_r.at[m])

    def put_sib(m, _):
        put(SIB_A + m, sib[m, 0])
        put(SIB_B + m, sib[m, 1])
        return 0

    lax.fori_loop(0, 5, put_sib, 0)

    def load_set(position, index):
        part = slice(position * B, (position + 1) * B)
        xs[part, :] = hl[index]
        xt[:, part] = hlt[index]

    def flip(i):
        return i + 1 - 2 * lax.rem(i, 2)

    low2 = lax.broadcasted_iota(jnp.int32, (2 * B, B), 1) < HD

    def run_pair(b, job):
        own, c1 = ((OWN_A, C1_A), (OWN_B, C1_B))[job]
        first = own + 2 * b
        side = c1 + flip(b)
        far = C2_A + flip(lax.div(b, 2)) if job == 0 else C2_O
        load_set(0, first)
        load_set(1, first + 1)
        load_set(2, side)
        load_set(3, far)
        landed(qgr, qg_r, first)
        landed(qgr, qg_r, first + 1)
        qg = qgr[rows(first * B, 2 * B), :]
        zero = jnp.zeros_like(qg)

        def halves(v):
            h = v.astype(BF16).astype(F32)
            return h, v - h

        h, l = halves(jnp.where(low2, qg * math.log2(math.e), qg))
        turned = pltpu.roll(h, HD, 1)
        rq = jnp.concatenate([jnp.where(low2, h, turned), jnp.where(low2, l, zero)], axis=1).astype(BF16)
        rg = jnp.concatenate([jnp.where(low2, zero, l), jnp.where(low2, turned, h)], axis=1).astype(BF16)
        sd[...] = dot(xs[:, 0 : 2 * B], rq, NT)
        dp[...] = dot(xs[:, B : 3 * B], rg, NT)
        top = jnp.full((8, 2 * B), -jnp.inf, F32)
        offsets = [float(max(i - 1, 0)) for i in range(9)]
        for i in range(9):
            s = sd[i * B : (i + 1) * B]
            top = jnp.maximum(top, jnp.max(s.reshape(16, 8, 2 * B), axis=0) + offsets[i])
        top = jnp.max(top, axis=0, keepdims=True)
        total = jnp.zeros((8, 2 * B), F32)
        along = jnp.zeros((8, 2 * B), F32)
        for i in range(9):
            part = slice(i * B, (i + 1) * B)
            e = jnp.exp2(sd[part] - (top - offsets[i]))
            sd[part] = e
            total = total + jnp.sum(e.reshape(16, 8, 2 * B), axis=0)
            along = along + jnp.sum((e * dp[part]).reshape(16, 8, 2 * B), axis=0)
        norm = 1.0 / jnp.sum(total, axis=0, keepdims=True)
        row_dot = jnp.sum(along, axis=0, keepdims=True) * norm
        for i in range(9):
            part = slice(i * B, (i + 1) * B)
            prob = sd[part] * norm
            ph[part], plo[part] = split(prob)
            dh[part], dl[part] = split(prob * (dp[part] - row_dot))

        dq = dot(xt[0:B], dh[...])
        dq = dq[0:HD] + dq[HD:B] + dot(xt[0:HD], dl[...])
        at = dot(xt[B : 2 * B], ph[...])
        at = at[0:HD] + at[HD:B] + dot(xt[B : B + HD], plo[...])
        rqa[rows(first * B, 2 * B), :] = jnp.concatenate([dq * 0.125, at], axis=0).T
        for s in range(2):
            send_back(block(rqa, first + s), fqa, rq_s, rq_r, first + s, job)

        h, l = halves(qg)
        rk = jnp.concatenate([jnp.where(low2, h, zero), jnp.where(low2, l, zero)], axis=1).astype(BF16)
        rv = jnp.concatenate([jnp.where(low2, zero, h), jnp.where(low2, zero, l)], axis=1).astype(BF16)
        high = dot(dh[...], rk) + dot(ph[...], rv)
        grads = high[:, 0:B] + high[:, B : 2 * B] + (dot(dl[...], rk[:, 0:B]) + dot(plo[...], rv[:, 0:B]))
        ga[rows(first * B, 2 * B), :] = grads[0 : 2 * B]
        ga[rows(side * B, B), :] = grads[2 * B : 3 * B]
        ga[rows(far * B, B), :] = ga[rows(far * B, B), :] + grads[3 * B : 4 * B]
        top_sets = slice((SIB_A, SIB_B)[job] * B, ((SIB_A, SIB_B)[job] + 5) * B)
        ga[top_sets] = ga[top_sets] + grads[4 * B :]

    def run_job(job, count):
        for m in range(5):
            load_set(4 + m, (SIB_A, SIB_B)[job] + m)

        def step(i, _):
            run_pair(i if job else lax.rem(t + 4 - turn(i, 4), 4), job)
            return 0

        lax.fori_loop(0, count, step, 0)

    def spread(src, dst, start, n):
        half = 0.5 * src
        for odd in range(2):
            at = pl.ds(start + odd, n, stride=2)
            dst[at, :] = dst[at, :] + half

    run_job(1, 2)
    gx_src = ga.at[pl.ds(C2_O * B, 6 * B)]
    gx = pltpu.make_async_remote_copy(gx_src, xr, gx_s, gx_r, device_id=other, device_id_type=MESH)
    gx.start()
    run_job(0, 4)
    gx.wait()
    for m in range(5):
        gs[m, 0] = ga[(SIB_A + m) * B : (SIB_A + m + 1) * B]
        gs[m, 1] = ga[(SIB_B + m) * B : (SIB_B + m + 1) * B] + xr[(1 + m) * B : (2 + m) * B]
        send_subtrees(m, lambda job, j, n: gs.at[m, job, rows(j * n, n), :], gr, gs_s, gs_r)

    for i in range(2):
        spread(ga[(C2_A + i) * B : (C2_A + i + 1) * B], ga, (C1_A + 2 * i) * B, B)
    for i in range(4):
        spread(ga[(C1_A + i) * B : (C1_A + i + 1) * B], ga, (OWN_A + 2 * i) * B, B)
    spread(xr[0:B], ga, C1_B * B, B)
    for i in range(2):
        spread(ga[(C1_B + i) * B : (C1_B + i + 1) * B], ga, (OWN_B + 2 * i) * B, B)
    both_jobs_round(lambda i, job: send_back(block(ga, i), fkv, rk_s, rk_r, i, job))

    ups = (u3, u4, u5, u6, u7)
    for m in (4, 3, 2, 1, 0):
        wait_all(gr.at[m], gs_r.at[m])
        n = B >> m
        for job in range(2):
            acc = gr[m, job, 0:n]
            for j in range(1, 2**m):
                acc = acc + gr[m, job, j * n : (j + 1) * n]
            ups[m][job] = acc
    for m in (4, 3, 2, 1):
        for job in range(2):
            spread(ups[m][job], ups[m - 1].at[job], 0, B >> m)
    both_jobs_round(lambda i, job: send_back(c3_part(i, job), fc3, rc_s, rc_r, i, job))

    sent_out(qgs, qg_s)
    cx.wait_send()
    for m in range(5):
        wait_all(sib.at[m], sb_s.at[m])
        wait_all(gr.at[m], gs_s.at[m])

    def finish(i, job):
        sent_back(block(rqa, i), rq_s, i, job)
        sent_back(block(ga, i), rk_s, i, job)
        sent_back(c3_part(i, job), rc_s, i, job)
        for dst, sem in ((fqa, rq_r), (fkv, rk_r), (fc3, rc_r)):
            pltpu.make_async_copy(dst.at[i], dst.at[i], sem.at[i]).wait()

    both_jobs(finish)


def unpack(qa, kv, c3, oa, oq, ok, ov):
    low = lax.broadcasted_iota(jnp.int32, (B, B), 1) < HD

    def pair(even, odd, first, last):
        first[...] = jnp.where(low, even, pltpu.roll(odd, HD, 1))
        last[...] = jnp.where(low, pltpu.roll(even, HD, 1), odd)

    def whole(h):
        above = jnp.broadcast_to(c3[h][:, None, :] * 0.125, (16, 8, B)).reshape(B, B)
        return kv[h] + above

    for i in range(3):
        cols = slice(i * B, (i + 1) * B)
        pair(qa[2 * i], qa[2 * i + 1], oq.at[:, cols], oa.at[:, cols])
        pair(whole(2 * i), whole(2 * i + 1), ok.at[:, cols], ov.at[:, cols])


def on_device(queries, keys, values, cotangent):
    hbm = pl.BlockSpec(memory_space=pl.ANY)
    dma = pltpu.SemaphoreType.DMA
    scratch = [pltpu.VMEM(queries.shape, F32)] * 4
    scratch += [
        pltpu.VMEM((12, B, B), F32),
        pltpu.VMEM((12, B, B), F32),
        pltpu.VMEM((SETS * B, B), F32),
        pltpu.VMEM((12 * B, B), F32),
        pltpu.VMEM((B, B), F32),
    ]
    scratch += [pltpu.VMEM((2, B >> m, B), F32) for m in range(5)]
    scratch += [
        pltpu.VMEM((5, 2, B, B), F32),
        pltpu.VMEM((SETS, B, 3 * B), BF16),
        pltpu.VMEM((SETS, 2 * B, B), BF16),
        pltpu.VMEM((9 * B, 3 * B), BF16),
        pltpu.VMEM((2 * B, 9 * B), BF16),
        pltpu.VMEM((9 * B, 2 * B), F32),
        pltpu.VMEM((9 * B, 2 * B), F32),
    ]
    scratch += [pltpu.VMEM((9 * B, 2 * B), BF16)] * 4
    scratch += [
        pltpu.VMEM((SETS * B, B), F32),
        pltpu.VMEM((6 * B, B), F32),
        pltpu.VMEM((5, 2, B, B), F32),
        pltpu.VMEM((5, 2, B, B), F32),
    ]
    scratch += [pltpu.VMEM((2, B >> m, B), F32) for m in range(5)]
    scratch += [
        pltpu.VMEM((12 * B, B), F32),
    ]
    scratch += [dma((4,))] + [dma((12,))] * 4 + [dma] * 2 + [dma((5,))] * 2 + [dma] * 2 + [dma((5,))] * 2
    scratch += [dma((12,))] * 6
    packed = pl.pallas_call(
        kernel,
        out_shape=[jax.ShapeDtypeStruct((12, n, B), F32) for n in (B, B, 16)],
        in_specs=[hbm] * 4,
        out_specs=[hbm] * 3,
        scratch_shapes=scratch,
        compiler_params=pltpu.CompilerParams(
            collective_id=0, has_side_effects=True, vmem_limit_bytes=56 * 2**20
        ),
    )(queries, keys, values, cotangent)
    return pl.pallas_call(
        unpack,
        grid=(HEADS // 6,),
        out_shape=[jax.ShapeDtypeStruct(queries.shape, F32)] * 4,
        in_specs=[pl.BlockSpec((6, n, B), lambda i: (i, 0, 0)) for n in (B, B, 16)],
        out_specs=[pl.BlockSpec((B, 3 * B), lambda i: (0, i))] * 4,
    )(*packed)


def solution(mesh):
    spec = P(("seqhi", "seqlo"), None)
    return jax.shard_map(
        on_device, mesh=mesh, in_specs=(spec,) * 4, out_specs=(spec,) * 4, check_vma=False
    )
```

```python
import functools
import math

import jax
import jax.numpy as jnp
from jax import lax
from jax.experimental import pallas as pl
from jax.experimental.pallas import tpu as pltpu
from jax.sharding import PartitionSpec as P

MESH = pl.DeviceIdType.MESH
F32 = jnp.float32
BF16 = jnp.bfloat16
HEADS = 12
HD = 64
B = 128
LOG_TWO = math.log(2.0)
NT = (((1,), (1,)), ((), ()))
NEAR = (0, 1, 7, 2, 6, 3, 5, 4)
LATE = (6, 3, 5, 4)

OWN_A, OWN_B, C1_A, C1_B, C2_A, SIB_A, C2_O, SIB_B, SETS = 0, 8, 12, 16, 18, 20, 25, 26, 31


def dot(a, b, dims=(((1,), (0,)), ((), ()))):
    return lax.dot_general(a, b, dims, preferred_element_type=F32)


def split(v):
    hi = v.astype(BF16)
    return hi, (v - hi.astype(F32)).astype(BF16)


def rows(start, count):
    return pl.ds(pl.multiple_of(start, 8), count)


def kernel(
    q_hbm, k_hbm, v_hbm, g_hbm,
    fqa, fkv, fc3,
    q_ref, k_ref, v_ref, g_ref,
    kvs, qgs, kvr, qgr, c2o, cs3, cs4, cs5, cs6, cs7, sib,
    hl, hlt, xs, xt, sd, dp, ph, plo, dh, dl, ga, xr, gs, gr, u3, u4, u5, u6, u7, nought, rqa,
    in_s, kv_s, kv_r, qg_s, qg_r, cx_s, cx_r, sb_s, sb_r, gx_s, gx_r, gs_s, gs_r,
    rq_s, rq_r, rk_s, rk_r, rc_s, rc_r,
):
    hi_id, lo_id = lax.axis_index("seqhi"), lax.axis_index("seqlo")
    x, k = lax.div(hi_id, 2), lax.rem(hi_id, 2)
    y, z = lax.div(lo_id, 8), lax.rem(lo_id, 8)
    t = lax.div(z, 2)
    cw = lax.rem(z, 2)
    quad = lax.div(z, 4)
    core_of = (k, cw)
    other = (x * 2 + 1 - k, lo_id)

    def flip(i):
        return i + 1 - 2 * lax.rem(i, 2)

    flip_z, flip_x, flip_y = flip(z), flip(x), flip(y)
    far_x, far_y = 2 * (1 - lax.div(x, 2)), 2 * (1 - lax.div(y, 2))

    def place(job, xx, turn, yy):
        if job == 0:
            return (xx * 2 + (1 - k if turn else k), yy * 8 + z)
        return (xx * 2 + k, yy * 8 + (flip_z if turn else z))

    def worker(u, j, shared):
        if shared:
            return quad, 2 * u + k
        return k, 2 * u + lax.div(j, 2)

    def owner(slot, job):
        if job == 0:
            return k, slot, 3 * t + 2 * cw
        return cw, 4 * k + slot - OWN_B, 3 * t + 1

    loads = [
        pltpu.make_async_copy(src, dst, in_s.at[i])
        for i, (src, dst) in enumerate(((k_hbm, k_ref), (v_hbm, v_ref), (q_hbm, q_ref), (g_hbm, g_ref)))
    ]
    for load in loads:
        load.start()

    barrier = pltpu.get_barrier_semaphore()

    def greet(dev):
        pl.semaphore_signal(barrier, inc=1, device_id=dev, device_id_type=MESH)

    def greet_unless_me(core, zz):
        @pl.when(jnp.logical_not((core == k) & (zz == z)))
        def _():
            greet((x * 2 + core, y * 8 + zz))

    def greet_ring(i, _):
        greet_unless_me(k, i)
        return 0

    def greet_shared(i, _):
        greet_unless_me(*worker(i, 1, True))
        greet_unless_me(*owner(OWN_B + i, 1)[:2])
        return 0

    lax.fori_loop(0, 8, greet_ring, 0)
    lax.fori_loop(0, 4, greet_shared, 0)
    for xx in range(4):
        for yy in range(4):
            greet(place(0, xx, True, yy))
            greet(place(1, xx, True, yy))

            @pl.when(jnp.logical_not((xx == x) & (yy == y)))
            def _():
                greet(place(0, xx, False, yy))

    low = lax.broadcasted_iota(jnp.int32, (B, B), 1) < HD

    def pack(a_ref, b_ref, dst, scale):
        for pair in range(HEADS // 2):
            cols = slice(pair * B, (pair + 1) * B)
            a, b = a_ref[:, cols], b_ref[:, cols]
            if scale != 1.0:
                a = a * scale
            dst[2 * pair] = jnp.where(low, a, pltpu.roll(b, HD, 1))
            dst[2 * pair + 1] = jnp.where(low, pltpu.roll(a, HD, 1), b)

    loads[0].wait()
    loads[1].wait()
    pack(k_ref, v_ref, kvs, 1.0)
    pl.semaphore_wait(barrier, 62 - 2 * (1 - lax.rem(cw + k, 2)) * (1 - lax.rem(quad + k, 2)))

    def turn(i, n):
        return lax.rem(i + k * (n - 2 * i) + n, n)

    def send_head(src, dst, ssem, rsem, u, j, shared=False):
        h = 3 * u + j
        wk, wz = worker(u, j, shared)
        slot = 8 + lax.rem(z, 4) if shared else z
        me = (wz == z) & (wk == k)

        @pl.when(me)
        def _():
            pltpu.make_async_copy(src.at[h], dst.at[rows(slot * B, B)], rsem.at[slot]).start()

        @pl.when(jnp.logical_not(me))
        def _():
            pltpu.make_async_remote_copy(
                src.at[h], dst.at[rows(slot * B, B)], ssem.at[h], rsem.at[slot],
                device_id=(x * 2 + wk, y * 8 + wz), device_id_type=MESH,
            ).start()

    def send_shared(src, dst, ssem, rsem):
        def step(i, _):
            send_head(src, dst, ssem, rsem, lax.rem(t + turn(i, 4), 4), 1, True)
            return 0

        lax.fori_loop(0, 4, step, 0)

    def send_own(src, dst, ssem, rsem):
        def step(i, _):
            u = lax.rem(t + turn(i, 4), 4)
            for j in (0, 2):
                send_head(src, dst, ssem, rsem, u, j)
            return 0

        lax.fori_loop(0, 4, step, 0)

    def send_own_near(src, dst, ssem, rsem):
        for d in NEAR:
            wz = lax.rem(z + d, 8)
            send_head(src, dst, ssem, rsem, lax.div(wz, 2), 2 * lax.rem(wz, 2))

    def sent_out(src, ssem):
        def step(u, _):
            for j in range(3):
                h = 3 * u + j
                wk, wz = worker(u, j, j == 1)

                @pl.when(jnp.logical_not((wz == z) & (wk == k)))
                def _():
                    pltpu.make_async_copy(src.at[h], src.at[h], ssem.at[h]).wait()
            return 0

        lax.fori_loop(0, 4, step, 0)

    def landed(dst, rsem, slot):
        part = dst.at[rows(slot * B, B)]
        pltpu.make_async_copy(part, part, rsem.at[slot]).wait()

    def send_back(part, dst, ssem, rsem, slot, job):
        oc, oz, h = owner(slot, job)
        me = (oc == k) & (oz == z)

        @pl.when(me)
        def _():
            pltpu.make_async_copy(part, dst.at[h], rsem).start()

        @pl.when(jnp.logical_not(me))
        def _():
            pltpu.make_async_remote_copy(
                part, dst.at[h], ssem.at[slot], rsem,
                device_id=(x * 2 + oc, y * 8 + oz), device_id_type=MESH,
            ).start()

    def sent_back(part, ssem, slot, job):
        oc, oz, _ = owner(slot, job)

        @pl.when(jnp.logical_not((oc == k) & (oz == z)))
        def _():
            pltpu.make_async_copy(part, part, ssem.at[slot]).wait()

    def block(ref, slot):
        return ref.at[rows(slot * B, B)]

    def c3_part(slot, job):
        return u3.at[job, rows(16 * owner(slot, job)[1], 16), :]

    def round_early(what):
        def shared(i, _):
            what(8 + lax.rem(z + i, 4), 1)
            return 0

        lax.fori_loop(0, 4, shared, 0)
        for d in NEAR:
            if d not in LATE:
                what(lax.rem(z + d, 8), 0)

    def both_jobs(what):
        for job, (first, last) in enumerate(((0, 8), (8, 12))):
            def step(i, _, job=job):
                what(i, job)
                return 0

            lax.fori_loop(first, last, step, 0)

    def sibling(m, turned):
        if m == 0:
            return [(0, x, False, flip_y)]
        if m == 1:
            return [(e, x, False, far_y + e) for e in range(2)]
        if m == 2:
            return [(yy, x, True, yy) for yy in range(4)]
        out = []
        for e in range(m - 2):
            for first in range(2):
                xx = flip_x if m == 3 else far_x + e
                out += [(e * 8 + 4 * first + yy, xx, first, yy) for yy in range(4)]
        return out

    def send_subtrees(m, src_part, dst, ssem, rsem, halved=False):
        n = B >> m
        for job in range(2):
            c = core_of[job]
            own = m + 5 * job if halved else m
            mine = lax.rem((x * 8 + c * 4 + y), 2**m) * n
            for j, xx, turned, yy in sibling(m, c):
                if m >= 3:
                    index = (j // 8) * 8 + lax.rem(c + (j // 4) % 2, 2) * 4 + j % 4
                else:
                    index = j
                at, count = (k * (n // 2), n // 2) if halved and job == 1 and m < 4 else (0, n)
                pltpu.make_async_remote_copy(
                    src_part(job, index * n + at, count), dst.at[m, job, rows(mine + at, count), :],
                    ssem.at[own], rsem.at[own],
                    device_id=place(job, xx, turned, yy), device_id_type=MESH,
                ).start()

    def wait_all(ref, sem):
        pltpu.make_async_copy(ref, ref, sem).wait()

    send_shared(kvs, kvr, kv_s, kv_r)
    send_own_near(kvs, kvr, kv_s, kv_r)
    loads[2].wait()
    loads[3].wait()
    pack(q_ref, g_ref, qgs, 0.125)
    for start, count in ((C2_A, SETS - C2_A),):
        ga[start * B : (start + count) * B] = jnp.zeros((count * B, B), F32)
    sent_out(kvs, kv_s)
    send_shared(qgs, qgr, qg_s, qg_r)

    def put(index, v):
        h = v.astype(BF16)
        hf = h.astype(F32)
        l = v - hf
        kk = jnp.where(low, hf, pltpu.roll(l, HD, 1))
        vv = jnp.where(low, pltpu.roll(hf, HD, 1), l)
        hl[index, :, 0:B] = kk.astype(BF16)
        hl[index, :, B : 2 * B] = h
        hl[index, :, 2 * B : 3 * B] = vv.astype(BF16)
        hlt[index, 0:B, :] = kk.T.astype(BF16)
        hlt[index, B : 2 * B, :] = vv.T.astype(BF16)

    def halve(ref, start, n):
        return 0.5 * (ref[pl.ds(start, n, stride=2), :] + ref[pl.ds(start + 1, n, stride=2), :])

    for s in range(OWN_B, 12):
        landed(kvr, kv_r, s)
    for i in range(2):
        kvr[(C1_B + i) * B : (C1_B + i + 1) * B] = halve(kvr, (OWN_B + 2 * i) * B, B)
    kvr[30 * B : 31 * B] = halve(kvr, C1_B * B, B)
    c2_mine = kvr.at[pl.ds(30 * B, B)]
    cx = pltpu.make_async_remote_copy(c2_mine, c2o, cx_s, cx_r, device_id=other, device_id_type=MESH)
    cx.start()
    for s in range(8):
        landed(kvr, kv_r, s)
    for i in range(4):
        kvr[(C1_A + i) * B : (C1_A + i + 1) * B] = halve(kvr, (OWN_A + 2 * i) * B, B)
    for i in range(2):
        kvr[(C2_A + i) * B : (C2_A + i + 1) * B] = halve(kvr, (C1_A + 2 * i) * B, B)
    cs3[0] = halve(kvr, C2_A * B, B)
    cs3[1, rows(64 * k, 64), :] = halve(kvr, 30 * B, 64)
    cx.wait_recv()
    cs3[1, rows(64 * (1 - k), 64), :] = halve(c2o, 0, 64)
    levels = (cs3, cs4, cs5, cs6, cs7)
    for m in range(5):
        if m:
            for job in range(2):
                levels[m][job] = halve(levels[m - 1].at[job], 0, B >> m)
        send_subtrees(m, lambda job, at, n: levels[m].at[job], sib, sb_s, sb_r)
    send_own(qgs, qgr, qg_s, qg_r)

    def put_step(i, _):
        put(i, kvr[rows(i * B, B), :])
        return 0

    lax.fori_loop(0, 20, put_step, 0)
    put(C2_O, c2o[...])
    for m in range(5):
        wait_all(sib.at[m], sb_r.at[m])
        put(SIB_B + m, sib[m, 1])

    def load_set(position, index):
        part = slice(position * B, (position + 1) * B)
        xs[part, :] = hl[index]
        xt[:, part] = hlt[index]

    low2 = lax.broadcasted_iota(jnp.int32, (2 * B, B), 1) < HD

    def run_pair(b, job):
        own, c1 = ((OWN_A, C1_A), (OWN_B, C1_B))[job]
        first = own + 2 * b
        side = c1 + flip(b)
        far = C2_A + flip(lax.div(b, 2)) if job == 0 else C2_O
        load_set(0, first)
        load_set(1, first + 1)
        load_set(2, side)
        load_set(3, far)
        landed(qgr, qg_r, first)
        landed(qgr, qg_r, first + 1)
        qg = qgr[rows(first * B, 2 * B), :]
        zero = jnp.zeros_like(qg)

        def halves(v):
            h = v.astype(BF16).astype(F32)
            return h, v - h

        h, l = halves(jnp.where(low2, qg * math.log2(math.e), qg))
        turned = pltpu.roll(h, HD, 1)
        rq = jnp.concatenate([jnp.where(low2, h, turned), jnp.where(low2, l, zero)], axis=1).astype(BF16)
        rg = jnp.concatenate([jnp.where(low2, zero, l), jnp.where(low2, turned, h)], axis=1).astype(BF16)
        sd[...] = dot(xs[:, 0 : 2 * B], rq, NT)
        dp[...] = dot(xs[:, B : 3 * B], rg, NT)
        top = jnp.full((8, 2 * B), -jnp.inf, F32)
        offsets = [float(max(i - 1, 0)) for i in range(9)]
        for i in range(9):
            s = sd[i * B : (i + 1) * B]
            top = jnp.maximum(top, jnp.max(s.reshape(16, 8, 2 * B), axis=0) + offsets[i])
        top = jnp.max(top, axis=0, keepdims=True)
        total = jnp.zeros((8, 2 * B), F32)
        along = jnp.zeros((8, 2 * B), F32)
        for i in range(9):
            part = slice(i * B, (i + 1) * B)
            e = jnp.exp2(sd[part] - (top - offsets[i]))
            sd[part] = e
            total = total + jnp.sum(e.reshape(16, 8, 2 * B), axis=0)
            along = along + jnp.sum((e * dp[part]).reshape(16, 8, 2 * B), axis=0)
        norm = 1.0 / jnp.sum(total, axis=0, keepdims=True)
        row_dot = jnp.sum(along, axis=0, keepdims=True) * norm
        for i in range(9):
            part = slice(i * B, (i + 1) * B)
            prob = sd[part] * norm
            ph[part], plo[part] = split(prob)
            dh[part], dl[part] = split(prob * (dp[part] - row_dot))

        dq = dot(xt[0:B], dh[...])
        dq = dq[0:HD] + dq[HD:B] + dot(xt[0:HD], dl[...])
        at = dot(xt[B : 2 * B], ph[...])
        at = at[0:HD] + at[HD:B] + dot(xt[B : B + HD], plo[...])
        rqa[rows(first * B, 2 * B), :] = jnp.concatenate([dq * 0.125, at], axis=0).T
        for s in range(2):
            send_back(block(rqa, first + s), fqa, rq_s, rq_r, first + s, job)

        h, l = halves(qg)
        rk = jnp.concatenate([jnp.where(low2, h, zero), jnp.where(low2, l, zero)], axis=1).astype(BF16)
        rv = jnp.concatenate([jnp.where(low2, zero, h), jnp.where(low2, zero, l)], axis=1).astype(BF16)
        high = dot(dh[...], rk) + dot(ph[...], rv)
        grads = high[:, 0:B] + high[:, B : 2 * B] + (dot(dl[...], rk[:, 0:B]) + dot(plo[...], rv[:, 0:B]))
        ga[rows(first * B, 2 * B), :] = grads[0 : 2 * B]
        ga[rows(side * B, B), :] = grads[2 * B : 3 * B]
        ga[rows(far * B, B), :] = ga[rows(far * B, B), :] + grads[3 * B : 4 * B]
        top_sets = slice((SIB_A, SIB_B)[job] * B, ((SIB_A, SIB_B)[job] + 5) * B)
        ga[top_sets] = ga[top_sets] + grads[4 * B :]

    def run_job(job, count):
        for m in range(5):
            if job == 0:
                put(SIB_A + m, sib[m, 0])
            load_set(4 + m, (SIB_A, SIB_B)[job] + m)

        def step(i, _):
            run_pair(i if job else lax.rem(t + 4 - turn(i, 4), 4), job)
            return 0

        lax.fori_loop(0, count, step, 0)

    def spread(src, dst, start, n):
        half = 0.5 * src
        for odd in range(2):
            at = pl.ds(start + odd, n, stride=2)
            dst[at, :] = dst[at, :] + half

    run_job(1, 2)
    gx_src = ga.at[pl.ds(C2_O * B, 6 * B)]
    gx = pltpu.make_async_remote_copy(gx_src, xr, gx_s, gx_r, device_id=other, device_id_type=MESH)
    gx.start()
    run_job(0, 4)
    gx.wait()
    for m in range(5):
        gs[m, 0] = ga[(SIB_A + m) * B : (SIB_A + m + 1) * B]
        gs[m, 1] = ga[(SIB_B + m) * B : (SIB_B + m + 1) * B] + xr[(1 + m) * B : (2 + m) * B]
        send_subtrees(m, lambda job, at, n: gs.at[m, job, rows(at, n), :], gr, gs_s, gs_r, True)

    for i in range(2):
        spread(ga[(C2_A + i) * B : (C2_A + i + 1) * B], ga, (C1_A + 2 * i) * B, B)
    for i in range(4):
        spread(ga[(C1_A + i) * B : (C1_A + i + 1) * B], ga, (OWN_A + 2 * i) * B, B)
    spread(xr[0:B], ga, C1_B * B, B)
    for i in range(2):
        spread(ga[(C1_B + i) * B : (C1_B + i + 1) * B], ga, (OWN_B + 2 * i) * B, B)
    def send_now(i, job):
        send_back(block(ga, i), fkv, rk_s, rk_r, i, job)

    round_early(send_now)

    nought[...] = jnp.zeros_like(nought)
    for d in LATE:
        wz = lax.rem(z + 8 - d, 8)
        pltpu.make_async_copy(nought, fc3.at[3 * lax.div(wz, 2) + 2 * lax.rem(wz, 2)], rc_r).start()


    def wait_halved(m, sem):
        wait_all(gr.at[m, 0], sem.at[m])
        wait_all(gr.at[m, 1] if m == 4 else gr.at[m, 1, 0:64], sem.at[5 + m])

    ups = (u3, u4, u5, u6, u7)
    for m in (4, 3, 2, 1, 0):
        wait_halved(m, gs_r)
        n = B >> m
        acc = gr[m, 0, 0:n]
        for j in range(1, 2**m):
            acc = acc + gr[m, 0, j * n : (j + 1) * n]
        ups[m][0] = acc
        at, count = (k * (n // 2), n // 2) if m < 4 else (0, n)
        acc = gr[m, 1, rows(at, count), :]
        for j in range(1, 2**m):
            acc = acc + gr[m, 1, rows(j * n + at, count), :]
        if m == 3:
            u6[1] = jnp.zeros((16, B), F32)
        ups[m][1, rows(at, count), :] = acc
    for m in (4, 3, 2, 1):
        n = B >> m
        spread(ups[m][0], ups[m - 1].at[0], 0, n)
        if m == 4:
            spread(u7[1], u6.at[1], 0, n)
        else:
            h = n // 2
            spread(ups[m][1, rows(k * h, h), :], ups[m - 1].at[1], 2 * k * h, h)

    def send_late(i, job):
        above = u3[job, rows(16 * owner(i, job)[1], 16), :] * 0.125
        part = rows(i * B, B)
        ga[part, :] = ga[part, :] + jnp.broadcast_to(above[:, None, :], (16, 8, B)).reshape(B, B)
        send_now(i, job)

    for d in LATE:
        send_late(lax.rem(z + d, 8), 0)
    round_early(lambda i, job: send_back(c3_part(i, job), fc3, rc_s, rc_r, i, job))

    sent_out(qgs, qg_s)
    cx.wait_send()
    for m in range(5):
        wait_all(sib.at[m], sb_s.at[m])
        wait_halved(m, gs_s)
    both_jobs(lambda i, job: sent_back(block(rqa, i), rq_s, i, job))
    wait_all(fqa, rq_r)

    def finish(i, job):
        sent_back(block(ga, i), rk_s, i, job)

    both_jobs(finish)
    round_early(lambda i, job: sent_back(c3_part(i, job), rc_s, i, job))
    wait_all(fkv, rk_r)
    wait_all(fc3, rc_r)


def unpack(qa, kv, c3, oa, oq, ok, ov):
    low = lax.broadcasted_iota(jnp.int32, (B, B), 1) < HD

    def pair(even, odd, first, last):
        first[...] = jnp.where(low, even, pltpu.roll(odd, HD, 1))
        last[...] = jnp.where(low, pltpu.roll(even, HD, 1), odd)

    def whole(h):
        above = jnp.broadcast_to(c3[h][:, None, :] * 0.125, (16, 8, B)).reshape(B, B)
        return kv[h] + above

    for i in range(3):
        cols = slice(i * B, (i + 1) * B)
        pair(qa[2 * i], qa[2 * i + 1], oq.at[:, cols], oa.at[:, cols])
        pair(whole(2 * i), whole(2 * i + 1), ok.at[:, cols], ov.at[:, cols])


def on_device(queries, keys, values, cotangent):
    hbm = pl.BlockSpec(memory_space=pl.ANY)
    dma = pltpu.SemaphoreType.DMA
    scratch = [pltpu.VMEM(queries.shape, F32)] * 4
    scratch += [
        pltpu.VMEM((12, B, B), F32),
        pltpu.VMEM((12, B, B), F32),
        pltpu.VMEM((SETS * B, B), F32),
        pltpu.VMEM((12 * B, B), F32),
        pltpu.VMEM((B, B), F32),
    ]
    scratch += [pltpu.VMEM((2, B >> m, B), F32) for m in range(5)]
    scratch += [
        pltpu.VMEM((5, 2, B, B), F32),
        pltpu.VMEM((SETS, B, 3 * B), BF16),
        pltpu.VMEM((SETS, 2 * B, B), BF16),
        pltpu.VMEM((9 * B, 3 * B), BF16),
        pltpu.VMEM((2 * B, 9 * B), BF16),
        pltpu.VMEM((9 * B, 2 * B), F32),
        pltpu.VMEM((9 * B, 2 * B), F32),
    ]
    scratch += [pltpu.VMEM((9 * B, 2 * B), BF16)] * 4
    scratch += [
        pltpu.VMEM((SETS * B, B), F32),
        pltpu.VMEM((6 * B, B), F32),
        pltpu.VMEM((5, 2, B, B), F32),
        pltpu.VMEM((5, 2, B, B), F32),
    ]
    scratch += [pltpu.VMEM((2, B >> m, B), F32) for m in range(5)]
    scratch += [
        pltpu.VMEM((16, B), F32),
        pltpu.VMEM((12 * B, B), F32),
    ]
    scratch += [dma((4,))] + [dma((12,))] * 4 + [dma] * 2 + [dma((5,))] * 2 + [dma] * 2 + [dma((10,))] * 2
    scratch += [dma((12,)), dma] * 3
    packed = pl.pallas_call(
        kernel,
        out_shape=[jax.ShapeDtypeStruct((12, n, B), F32) for n in (B, B, 16)],
        in_specs=[hbm] * 4,
        out_specs=[hbm] * 3,
        scratch_shapes=scratch,
        compiler_params=pltpu.CompilerParams(
            collective_id=0, has_side_effects=True, vmem_limit_bytes=56 * 2**20
        ),
    )(queries, keys, values, cotangent)
    return pl.pallas_call(
        unpack,
        grid=(HEADS // 6,),
        out_shape=[jax.ShapeDtypeStruct(queries.shape, F32)] * 4,
        in_specs=[pl.BlockSpec((6, n, B), lambda i: (i, 0, 0)) for n in (B, B, 16)],
        out_specs=[pl.BlockSpec((B, 3 * B), lambda i: (0, i))] * 4,
    )(*packed)


def solution(mesh):
    spec = P(("seqhi", "seqlo"), None)
    return jax.shard_map(
        on_device, mesh=mesh, in_specs=(spec,) * 4, out_specs=(spec,) * 4, check_vma=False
    )
```

```python
import functools
import math

import jax
import jax.numpy as jnp
from jax import lax
from jax.experimental import pallas as pl
from jax.experimental.pallas import tpu as pltpu
from jax.sharding import PartitionSpec as P

MESH = pl.DeviceIdType.MESH
F32 = jnp.float32
BF16 = jnp.bfloat16
HEADS = 12
HD = 64
B = 128
LOG_TWO = math.log(2.0)
NT = (((1,), (1,)), ((), ()))
NEAR = (0, 1, 7, 2, 6, 3, 5, 4)
LATE = (3, 5, 4)

OWN_A, OWN_B, C1_A, C1_B, C2_A, SIB_A, C2_O, SIB_B, SETS = 0, 8, 12, 16, 18, 20, 25, 26, 31


def dot(a, b, dims=(((1,), (0,)), ((), ()))):
    return lax.dot_general(a, b, dims, preferred_element_type=F32)


def split(v):
    hi = v.astype(BF16)
    return hi, (v - hi.astype(F32)).astype(BF16)


def rows(start, count):
    return pl.ds(pl.multiple_of(start, 8), count)


def kernel(
    q_hbm, k_hbm, v_hbm, g_hbm,
    fqa, fkv, fc3,
    q_ref, k_ref, v_ref, g_ref,
    kvs, qgs, kvr, qgr, c2o, cs3, cs4, cs5, cs6, cs7, sib,
    hl, hlt, xs, xt, sd, dp, ph, plo, dh, dl, ga, xr, gs, gr, u3, u4, u5, u6, u7, nought, rqa,
    in_s, kv_s, kv_r, qg_s, qg_r, cx_s, cx_r, sb_s, sb_r, gx_s, gx_r, gs_s, gs_r,
    rq_s, rq_r, rk_s, rk_r, rc_s, rc_r,
):
    hi_id, lo_id = lax.axis_index("seqhi"), lax.axis_index("seqlo")
    x, k = lax.div(hi_id, 2), lax.rem(hi_id, 2)
    y, z = lax.div(lo_id, 8), lax.rem(lo_id, 8)
    t = lax.div(z, 2)
    cw = lax.rem(z, 2)
    quad = lax.div(z, 4)
    core_of = (k, cw)
    other = (x * 2 + 1 - k, lo_id)

    def flip(i):
        return i + 1 - 2 * lax.rem(i, 2)

    flip_z, flip_x, flip_y = flip(z), flip(x), flip(y)
    far_x, far_y = 2 * (1 - lax.div(x, 2)), 2 * (1 - lax.div(y, 2))

    def place(job, xx, turn, yy):
        if job == 0:
            return (xx * 2 + (1 - k if turn else k), yy * 8 + z)
        return (xx * 2 + k, yy * 8 + (flip_z if turn else z))

    def worker(u, j, shared):
        if shared:
            return quad, 2 * u + k
        return k, 2 * u + lax.div(j, 2)

    def owner(slot, job):
        if job == 0:
            return k, slot, 3 * t + 2 * cw
        return cw, 4 * k + slot - OWN_B, 3 * t + 1

    loads = [
        pltpu.make_async_copy(src, dst, in_s.at[i])
        for i, (src, dst) in enumerate(((k_hbm, k_ref), (v_hbm, v_ref), (q_hbm, q_ref), (g_hbm, g_ref)))
    ]
    for load in loads:
        load.start()

    barrier = pltpu.get_barrier_semaphore()

    def greet(dev):
        pl.semaphore_signal(barrier, inc=1, device_id=dev, device_id_type=MESH)

    def greet_unless_me(core, zz):
        @pl.when(jnp.logical_not((core == k) & (zz == z)))
        def _():
            greet((x * 2 + core, y * 8 + zz))

    def greet_ring(i, _):
        greet_unless_me(k, i)
        return 0

    def greet_shared(i, _):
        greet_unless_me(*worker(i, 1, True))
        greet_unless_me(*owner(OWN_B + i, 1)[:2])
        return 0

    lax.fori_loop(0, 8, greet_ring, 0)
    lax.fori_loop(0, 4, greet_shared, 0)
    for xx in range(4):
        for yy in range(4):
            greet(place(0, xx, True, yy))
            greet(place(1, xx, True, yy))

            @pl.when(jnp.logical_not((xx == x) & (yy == y)))
            def _():
                greet(place(0, xx, False, yy))

    low = lax.broadcasted_iota(jnp.int32, (B, B), 1) < HD

    def pack(a_ref, b_ref, dst, scale):
        for pair in range(HEADS // 2):
            cols = slice(pair * B, (pair + 1) * B)
            a, b = a_ref[:, cols], b_ref[:, cols]
            if scale != 1.0:
                a = a * scale
            dst[2 * pair] = jnp.where(low, a, pltpu.roll(b, HD, 1))
            dst[2 * pair + 1] = jnp.where(low, pltpu.roll(a, HD, 1), b)

    loads[0].wait()
    loads[1].wait()
    pack(k_ref, v_ref, kvs, 1.0)
    pl.semaphore_wait(barrier, 62 - 2 * (1 - lax.rem(cw + k, 2)) * (1 - lax.rem(quad + k, 2)))

    def turn(i, n):
        return lax.rem(i + k * (n - 2 * i) + n, n)

    def send_head(src, dst, ssem, rsem, u, j, shared=False):
        h = 3 * u + j
        wk, wz = worker(u, j, shared)
        slot = 8 + lax.rem(z, 4) if shared else z
        me = (wz == z) & (wk == k)

        @pl.when(me)
        def _():
            pltpu.make_async_copy(src.at[h], dst.at[rows(slot * B, B)], rsem.at[slot]).start()

        @pl.when(jnp.logical_not(me))
        def _():
            pltpu.make_async_remote_copy(
                src.at[h], dst.at[rows(slot * B, B)], ssem.at[h], rsem.at[slot],
                device_id=(x * 2 + wk, y * 8 + wz), device_id_type=MESH,
            ).start()

    def send_shared(src, dst, ssem, rsem):
        def step(i, _):
            send_head(src, dst, ssem, rsem, lax.rem(t + turn(i, 4), 4), 1, True)
            return 0

        lax.fori_loop(0, 4, step, 0)

    def send_own(src, dst, ssem, rsem):
        def step(i, _):
            u = lax.rem(t + turn(i, 4), 4)
            for j in (0, 2):
                send_head(src, dst, ssem, rsem, u, j)
            return 0

        lax.fori_loop(0, 4, step, 0)

    def send_own_near(src, dst, ssem, rsem):
        for d in NEAR:
            wz = lax.rem(z + d, 8)
            send_head(src, dst, ssem, rsem, lax.div(wz, 2), 2 * lax.rem(wz, 2))

    def sent_out(src, ssem):
        def step(u, _):
            for j in range(3):
                h = 3 * u + j
                wk, wz = worker(u, j, j == 1)

                @pl.when(jnp.logical_not((wz == z) & (wk == k)))
                def _():
                    pltpu.make_async_copy(src.at[h], src.at[h], ssem.at[h]).wait()
            return 0

        lax.fori_loop(0, 4, step, 0)

    def landed(dst, rsem, slot):
        part = dst.at[rows(slot * B, B)]
        pltpu.make_async_copy(part, part, rsem.at[slot]).wait()

    def send_back(part, dst, ssem, rsem, slot, job):
        oc, oz, h = owner(slot, job)
        me = (oc == k) & (oz == z)

        @pl.when(me)
        def _():
            pltpu.make_async_copy(part, dst.at[h], rsem).start()

        @pl.when(jnp.logical_not(me))
        def _():
            pltpu.make_async_remote_copy(
                part, dst.at[h], ssem.at[slot], rsem,
                device_id=(x * 2 + oc, y * 8 + oz), device_id_type=MESH,
            ).start()

    def sent_back(part, ssem, slot, job):
        oc, oz, _ = owner(slot, job)

        @pl.when(jnp.logical_not((oc == k) & (oz == z)))
        def _():
            pltpu.make_async_copy(part, part, ssem.at[slot]).wait()

    def block(ref, slot):
        return ref.at[rows(slot * B, B)]

    def c3_part(slot, job):
        return u3.at[job, rows(16 * owner(slot, job)[1], 16), :]

    def round_early(what):
        for d in NEAR:
            if d not in LATE:
                what(lax.rem(z + d, 8), 0)

    def both_jobs(what):
        for job, (first, last) in enumerate(((0, 8), (8, 12))):
            def step(i, _, job=job):
                what(i, job)
                return 0

            lax.fori_loop(first, last, step, 0)

    def sibling(m, turned):
        if m == 0:
            return [(0, x, False, flip_y)]
        if m == 1:
            return [(e, x, False, far_y + e) for e in range(2)]
        if m == 2:
            return [(yy, x, True, yy) for yy in range(4)]
        out = []
        for e in range(m - 2):
            for first in range(2):
                xx = flip_x if m == 3 else far_x + e
                out += [(e * 8 + 4 * first + yy, xx, first, yy) for yy in range(4)]
        return out

    def send_subtrees(m, src_part, dst, ssem, rsem, halved=False):
        n = B >> m
        for job in range(2):
            c = core_of[job]
            own = m + 5 * job if halved else m
            mine = lax.rem((x * 8 + c * 4 + y), 2**m) * n
            for j, xx, turned, yy in sibling(m, c):
                if m >= 3:
                    index = (j // 8) * 8 + lax.rem(c + (j // 4) % 2, 2) * 4 + j % 4
                else:
                    index = j
                at, count = (k * (n // 2), n // 2) if halved and job == 1 and m < 4 else (0, n)
                pltpu.make_async_remote_copy(
                    src_part(job, index * n + at, count), dst.at[m, job, rows(mine + at, count), :],
                    ssem.at[own], rsem.at[own],
                    device_id=place(job, xx, turned, yy), device_id_type=MESH,
                ).start()

    def wait_all(ref, sem):
        pltpu.make_async_copy(ref, ref, sem).wait()

    send_shared(kvs, kvr, kv_s, kv_r)
    send_own_near(kvs, kvr, kv_s, kv_r)
    loads[2].wait()
    loads[3].wait()
    pack(q_ref, g_ref, qgs, 0.125)
    for start, count in ((C2_A, SETS - C2_A),):
        ga[start * B : (start + count) * B] = jnp.zeros((count * B, B), F32)
    sent_out(kvs, kv_s)
    send_shared(qgs, qgr, qg_s, qg_r)

    def put(index, v):
        h = v.astype(BF16)
        hf = h.astype(F32)
        l = v - hf
        kk = jnp.where(low, hf, pltpu.roll(l, HD, 1))
        vv = jnp.where(low, pltpu.roll(hf, HD, 1), l)
        hl[index, :, 0:B] = kk.astype(BF16)
        hl[index, :, B : 2 * B] = h
        hl[index, :, 2 * B : 3 * B] = vv.astype(BF16)
        hlt[index, 0:B, :] = kk.T.astype(BF16)
        hlt[index, B : 2 * B, :] = vv.T.astype(BF16)

    def halve(ref, start, n):
        return 0.5 * (ref[pl.ds(start, n, stride=2), :] + ref[pl.ds(start + 1, n, stride=2), :])

    for s in range(OWN_B, 12):
        landed(kvr, kv_r, s)
    for i in range(2):
        kvr[(C1_B + i) * B : (C1_B + i + 1) * B] = halve(kvr, (OWN_B + 2 * i) * B, B)
    kvr[30 * B : 31 * B] = halve(kvr, C1_B * B, B)
    c2_mine = kvr.at[pl.ds(30 * B, B)]
    cx = pltpu.make_async_remote_copy(c2_mine, c2o.at[pl.ds(0, B)], cx_s, cx_r, device_id=other, device_id_type=MESH)
    cx.start()
    for s in range(8):
        landed(kvr, kv_r, s)
    for i in range(4):
        kvr[(C1_A + i) * B : (C1_A + i + 1) * B] = halve(kvr, (OWN_A + 2 * i) * B, B)
    for i in range(2):
        kvr[(C2_A + i) * B : (C2_A + i + 1) * B] = halve(kvr, (C1_A + 2 * i) * B, B)
    cs3[0] = halve(kvr, C2_A * B, B)
    cs3[1, rows(64 * k, 64), :] = halve(kvr, 30 * B, 64)
    cx.wait_recv()
    cs3[1, rows(64 * (1 - k), 64), :] = halve(c2o, 0, 64)
    levels = (cs3, cs4, cs5, cs6, cs7)
    for m in range(5):
        if m:
            for job in range(2):
                levels[m][job] = halve(levels[m - 1].at[job], 0, B >> m)
        send_subtrees(m, lambda job, at, n: levels[m].at[job], sib, sb_s, sb_r)
    send_own(qgs, qgr, qg_s, qg_r)

    def put_step(i, _):
        put(i, kvr[rows(i * B, B), :])
        return 0

    lax.fori_loop(0, 20, put_step, 0)
    put(C2_O, c2o[0:B])
    for m in range(5):
        wait_all(sib.at[m], sb_r.at[m])
        put(SIB_B + m, sib[m, 1])

    def load_set(position, index):
        part = slice(position * B, (position + 1) * B)
        xs[part, :] = hl[index]
        xt[:, part] = hlt[index]

    low2 = lax.broadcasted_iota(jnp.int32, (2 * B, B), 1) < HD

    def run_pair(b, job):
        own, c1 = ((OWN_A, C1_A), (OWN_B, C1_B))[job]
        first = own + 2 * b
        side = c1 + flip(b)
        far = C2_A + flip(lax.div(b, 2)) if job == 0 else C2_O
        load_set(0, first)
        load_set(1, first + 1)
        load_set(2, side)
        load_set(3, far)
        landed(qgr, qg_r, first)
        landed(qgr, qg_r, first + 1)
        qg = qgr[rows(first * B, 2 * B), :]
        zero = jnp.zeros_like(qg)

        def halves(v):
            h = v.astype(BF16).astype(F32)
            return h, v - h

        h, l = halves(jnp.where(low2, qg * math.log2(math.e), qg))
        turned = pltpu.roll(h, HD, 1)
        rq = jnp.concatenate([jnp.where(low2, h, turned), jnp.where(low2, l, zero)], axis=1).astype(BF16)
        rg = jnp.concatenate([jnp.where(low2, zero, l), jnp.where(low2, turned, h)], axis=1).astype(BF16)
        sd[...] = dot(xs[:, 0 : 2 * B], rq, NT)
        dp[...] = dot(xs[:, B : 3 * B], rg, NT)
        top = jnp.full((8, 2 * B), -jnp.inf, F32)
        offsets = [float(max(i - 1, 0)) for i in range(9)]
        for i in range(9):
            s = sd[i * B : (i + 1) * B]
            top = jnp.maximum(top, jnp.max(s.reshape(16, 8, 2 * B), axis=0) + offsets[i])
        top = jnp.max(top, axis=0, keepdims=True)
        total = jnp.zeros((8, 2 * B), F32)
        along = jnp.zeros((8, 2 * B), F32)
        for i in range(9):
            part = slice(i * B, (i + 1) * B)
            e = jnp.exp2(sd[part] - (top - offsets[i]))
            sd[part] = e
            total = total + jnp.sum(e.reshape(16, 8, 2 * B), axis=0)
            along = along + jnp.sum((e * dp[part]).reshape(16, 8, 2 * B), axis=0)
        norm = 1.0 / jnp.sum(total, axis=0, keepdims=True)
        row_dot = jnp.sum(along, axis=0, keepdims=True) * norm
        for i in range(9):
            part = slice(i * B, (i + 1) * B)
            prob = sd[part] * norm
            ph[part], plo[part] = split(prob)
            dh[part], dl[part] = split(prob * (dp[part] - row_dot))

        dq = dot(xt[0:B], dh[...])
        dq = dq[0:HD] + dq[HD:B] + dot(xt[0:HD], dl[...])
        at = dot(xt[B : 2 * B], ph[...])
        at = at[0:HD] + at[HD:B] + dot(xt[B : B + HD], plo[...])
        rqa[rows(first * B, 2 * B), :] = jnp.concatenate([dq * 0.125, at], axis=0).T
        for s in range(2):
            send_back(block(rqa, first + s), fqa, rq_s, rq_r, first + s, job)

        h, l = halves(qg)
        rk = jnp.concatenate([jnp.where(low2, h, zero), jnp.where(low2, l, zero)], axis=1).astype(BF16)
        rv = jnp.concatenate([jnp.where(low2, zero, h), jnp.where(low2, zero, l)], axis=1).astype(BF16)
        high = dot(dh[...], rk) + dot(ph[...], rv)
        grads = high[:, 0:B] + high[:, B : 2 * B] + (dot(dl[...], rk[:, 0:B]) + dot(plo[...], rv[:, 0:B]))
        ga[rows(first * B, 2 * B), :] = grads[0 : 2 * B]
        ga[rows(side * B, B), :] = grads[2 * B : 3 * B]
        ga[rows(far * B, B), :] = ga[rows(far * B, B), :] + grads[3 * B : 4 * B]
        top_sets = slice((SIB_A, SIB_B)[job] * B, ((SIB_A, SIB_B)[job] + 5) * B)
        ga[top_sets] = ga[top_sets] + grads[4 * B :]

    def run_job(job, count):
        for m in range(5):
            if job == 0:
                put(SIB_A + m, sib[m, 0])
            load_set(4 + m, (SIB_A, SIB_B)[job] + m)

        def step(i, _):
            run_pair(i if job else lax.rem(t + 4 - turn(i, 4), 4), job)
            return 0

        lax.fori_loop(0, count, step, 0)

    def spread(src, dst, start, n):
        half = 0.5 * src
        for odd in range(2):
            at = pl.ds(start + odd, n, stride=2)
            dst[at, :] = dst[at, :] + half

    run_job(1, 2)
    gx_src = ga.at[pl.ds(C2_O * B, 6 * B)]
    gx = pltpu.make_async_remote_copy(gx_src, xr, gx_s, gx_r, device_id=other, device_id_type=MESH)
    gx.start()
    run_job(0, 4)
    gx.wait()
    for m in range(5):
        gs[m, 0] = ga[(SIB_A + m) * B : (SIB_A + m + 1) * B]
        gs[m, 1] = ga[(SIB_B + m) * B : (SIB_B + m + 1) * B] + xr[(1 + m) * B : (2 + m) * B]
        send_subtrees(m, lambda job, at, n: gs.at[m, job, rows(at, n), :], gr, gs_s, gs_r, True)

    for i in range(2):
        spread(ga[(C2_A + i) * B : (C2_A + i + 1) * B], ga, (C1_A + 2 * i) * B, B)
    for i in range(4):
        spread(ga[(C1_A + i) * B : (C1_A + i + 1) * B], ga, (OWN_A + 2 * i) * B, B)
    spread(xr[0:B], ga, C1_B * B, B)
    for i in range(2):
        spread(ga[(C1_B + i) * B : (C1_B + i + 1) * B], ga, (OWN_B + 2 * i) * B, B)
    def send_now(i, job):
        send_back(block(ga, i), fkv, rk_s, rk_r, i, job)

    round_early(send_now)

    nought[...] = jnp.zeros_like(nought)
    for u in range(4):
        pltpu.make_async_copy(nought, fc3.at[3 * u + 1], rc_r).start()
    for d in LATE:
        wz = lax.rem(z + 8 - d, 8)
        pltpu.make_async_copy(nought, fc3.at[3 * lax.div(wz, 2) + 2 * lax.rem(wz, 2)], rc_r).start()


    def wait_halved(m, sem):
        wait_all(gr.at[m, 0], sem.at[m])
        wait_all(gr.at[m, 1] if m == 4 else gr.at[m, 1, 0:64], sem.at[5 + m])

    ups = (u3, u4, u5, u6, u7)
    for m in (4, 3, 2, 1, 0):
        wait_halved(m, gs_r)
        n = B >> m
        acc = gr[m, 0, 0:n]
        for j in range(1, 2**m):
            acc = acc + gr[m, 0, j * n : (j + 1) * n]
        ups[m][0] = acc
        at, count = (k * (n // 2), n // 2) if m < 4 else (0, n)
        acc = gr[m, 1, rows(at, count), :]
        for j in range(1, 2**m):
            acc = acc + gr[m, 1, rows(j * n + at, count), :]
        if m == 3:
            u6[1] = jnp.zeros((16, B), F32)
        ups[m][1, rows(at, count), :] = acc
    for m in (4, 3, 2, 1):
        n = B >> m
        spread(ups[m][0], ups[m - 1].at[0], 0, n)
        if m == 4:
            spread(u7[1], u6.at[1], 0, n)
        else:
            h = n // 2
            spread(ups[m][1, rows(k * h, h), :], ups[m - 1].at[1], 2 * k * h, h)

    def send_late(i, job):
        above = u3[job, rows(16 * owner(i, job)[1], 16), :] * 0.125
        part = rows(i * B, B)
        ga[part, :] = ga[part, :] + jnp.broadcast_to(above[:, None, :], (16, 8, B)).reshape(B, B)
        send_now(i, job)

    def late_shared(i, _):
        send_late(8 + lax.rem(z + i, 4), 1)
        return 0

    lax.fori_loop(0, 4, late_shared, 0)
    for d in LATE:
        send_late(lax.rem(z + d, 8), 0)
    round_early(lambda i, job: send_back(c3_part(i, job), fc3, rc_s, rc_r, i, job))

    sent_out(qgs, qg_s)
    cx.wait_send()
    for m in range(5):
        wait_all(sib.at[m], sb_s.at[m])
        wait_halved(m, gs_s)
    both_jobs(lambda i, job: sent_back(block(rqa, i), rq_s, i, job))
    wait_all(fqa, rq_r)

    def finish(i, job):
        sent_back(block(ga, i), rk_s, i, job)

    both_jobs(finish)
    round_early(lambda i, job: sent_back(c3_part(i, job), rc_s, i, job))
    wait_all(fkv, rk_r)
    wait_all(fc3, rc_r)


def unpack(qa, kv, c3, oa, oq, ok, ov):
    low = lax.broadcasted_iota(jnp.int32, (B, B), 1) < HD

    def pair(even, odd, first, last):
        first[...] = jnp.where(low, even, pltpu.roll(odd, HD, 1))
        last[...] = jnp.where(low, pltpu.roll(even, HD, 1), odd)

    def whole(h):
        above = jnp.broadcast_to(c3[h][:, None, :] * 0.125, (16, 8, B)).reshape(B, B)
        return kv[h] + above

    for i in range(3):
        cols = slice(i * B, (i + 1) * B)
        pair(qa[2 * i], qa[2 * i + 1], oq.at[:, cols], oa.at[:, cols])
        pair(whole(2 * i), whole(2 * i + 1), ok.at[:, cols], ov.at[:, cols])


def on_device(queries, keys, values, cotangent):
    hbm = pl.BlockSpec(memory_space=pl.ANY)
    dma = pltpu.SemaphoreType.DMA
    scratch = [pltpu.VMEM(queries.shape, F32)] * 4
    scratch += [
        pltpu.VMEM((12, B, B), F32),
        pltpu.VMEM((12, B, B), F32),
        pltpu.VMEM(((SETS + 1) * B, B), F32),
        pltpu.VMEM((12 * B, B), F32),
        pltpu.VMEM((2 * B, B), F32),
    ]
    scratch += [pltpu.VMEM((3, B >> m, B), F32) for m in range(5)]
    scratch += [
        pltpu.VMEM((5, 2, B, B), F32),
        pltpu.VMEM((SETS, B, 3 * B), BF16),
        pltpu.VMEM((SETS, 2 * B, B), BF16),
        pltpu.VMEM((9 * B, 3 * B), BF16),
        pltpu.VMEM((2 * B, 9 * B), BF16),
        pltpu.VMEM((9 * B, 2 * B), F32),
        pltpu.VMEM((9 * B, 2 * B), F32),
    ]
    scratch += [pltpu.VMEM((9 * B, 2 * B), BF16)] * 4
    scratch += [
        pltpu.VMEM((SETS * B, B), F32),
        pltpu.VMEM((6 * B, B), F32),
        pltpu.VMEM((5, 2, B, B), F32),
        pltpu.VMEM((5, 2, B, B), F32),
    ]
    scratch += [pltpu.VMEM((3, B >> m, B), F32) for m in range(5)]
    scratch += [
        pltpu.VMEM((16, B), F32),
        pltpu.VMEM((12 * B, B), F32),
    ]
    scratch += [dma((4,))] + [dma((12,))] * 4 + [dma] * 2 + [dma((5,))] * 2 + [dma] * 2 + [dma((10,))] * 2
    scratch += [dma((12,)), dma] * 3
    packed = pl.pallas_call(
        kernel,
        out_shape=[jax.ShapeDtypeStruct((12, n, B), F32) for n in (B, B, 16)],
        in_specs=[hbm] * 4,
        out_specs=[hbm] * 3,
        scratch_shapes=scratch,
        compiler_params=pltpu.CompilerParams(
            collective_id=0, has_side_effects=True, vmem_limit_bytes=56 * 2**20
        ),
    )(queries, keys, values, cotangent)
    return pl.pallas_call(
        unpack,
        grid=(HEADS // 6,),
        out_shape=[jax.ShapeDtypeStruct(queries.shape, F32)] * 4,
        in_specs=[pl.BlockSpec((6, n, B), lambda i: (i, 0, 0)) for n in (B, B, 16)],
        out_specs=[pl.BlockSpec((B, 3 * B), lambda i: (0, i))] * 4,
    )(*packed)


def solution(mesh):
    spec = P(("seqhi", "seqlo"), None)
    return jax.shard_map(
        on_device, mesh=mesh, in_specs=(spec,) * 4, out_specs=(spec,) * 4, check_vma=False
    )
```

```python
import functools
import math

import jax
import jax.numpy as jnp
from jax import lax
from jax.experimental import pallas as pl
from jax.experimental.pallas import tpu as pltpu
from jax.sharding import PartitionSpec as P

MESH = pl.DeviceIdType.MESH
F32 = jnp.float32
BF16 = jnp.bfloat16
HEADS = 12
HD = 64
B = 128
LOG_TWO = math.log(2.0)
NT = (((1,), (1,)), ((), ()))
NEAR = (0, 1, 7, 2, 6, 3, 5, 4)
LATE = (3, 5, 4)

OWN_A, OWN_B, C1_A, C1_B, C2_A, SIB_A, C2_O, SIB_B, SETS = 0, 8, 12, 16, 18, 20, 25, 26, 31


def dot(a, b, dims=(((1,), (0,)), ((), ()))):
    return lax.dot_general(a, b, dims, preferred_element_type=F32)


def split(v):
    hi = v.astype(BF16)
    return hi, (v - hi.astype(F32)).astype(BF16)


def rows(start, count):
    return pl.ds(pl.multiple_of(start, 8), count)


def kernel(
    q_hbm, k_hbm, v_hbm, g_hbm,
    fqa, fkv, fc3,
    q_ref, k_ref, v_ref, g_ref,
    kvs, qgs, kvr, qgr, c2o, cs3, cs4, cs5, cs6, cs7, sib,
    hl, hlt, xs, xt, sd, dp, ph, plo, dh, dl, ga, xr, gs, gr, u3, u4, u5, u6, u7, nought, rqa,
    in_s, kv_s, kv_r, qg_s, qg_r, cx_s, cx_r, sb_s, sb_r, gx_s, gx_r, gs_s, gs_r,
    rq_s, rq_r, rk_s, rk_r, rc_s, rc_r,
):
    hi_id, lo_id = lax.axis_index("seqhi"), lax.axis_index("seqlo")
    x, k = lax.div(hi_id, 2), lax.rem(hi_id, 2)
    y, z = lax.div(lo_id, 8), lax.rem(lo_id, 8)
    t = lax.div(z, 2)
    cw = lax.rem(z, 2)
    quad = lax.div(z, 4)
    core_of = (k, cw)
    other = (x * 2 + 1 - k, lo_id)

    def flip(i):
        return i + 1 - 2 * lax.rem(i, 2)

    flip_z, flip_x, flip_y = flip(z), flip(x), flip(y)
    far_x, far_y = 2 * (1 - lax.div(x, 2)), 2 * (1 - lax.div(y, 2))

    def place(job, xx, turn, yy):
        if job == 0:
            return (xx * 2 + (1 - k if turn else k), yy * 8 + z)
        return (xx * 2 + k, yy * 8 + (flip_z if turn else z))

    def worker(u, j, shared):
        if shared:
            return quad, 2 * u + k
        return k, 2 * u + lax.div(j, 2)

    def owner(slot, job):
        if job == 0:
            return k, slot, 3 * t + 2 * cw
        return cw, 4 * k + slot - OWN_B, 3 * t + 1

    loads = [
        pltpu.make_async_copy(src, dst, in_s.at[i])
        for i, (src, dst) in enumerate(((k_hbm, k_ref), (v_hbm, v_ref), (q_hbm, q_ref), (g_hbm, g_ref)))
    ]
    for load in loads:
        load.start()

    barrier = pltpu.get_barrier_semaphore()

    def greet(dev):
        pl.semaphore_signal(barrier, inc=1, device_id=dev, device_id_type=MESH)

    def greet_unless_me(core, zz):
        @pl.when(jnp.logical_not((core == k) & (zz == z)))
        def _():
            greet((x * 2 + core, y * 8 + zz))

    def greet_ring(i, _):
        greet_unless_me(k, i)
        return 0

    def greet_shared(i, _):
        greet_unless_me(*worker(i, 1, True))
        greet_unless_me(*owner(OWN_B + i, 1)[:2])
        return 0

    lax.fori_loop(0, 8, greet_ring, 0)
    lax.fori_loop(0, 4, greet_shared, 0)
    for xx in range(4):
        for yy in range(4):
            greet(place(0, xx, True, yy))
            greet(place(1, xx, True, yy))

            @pl.when(jnp.logical_not((xx == x) & (yy == y)))
            def _():
                greet(place(0, xx, False, yy))

    low = lax.broadcasted_iota(jnp.int32, (B, B), 1) < HD

    def pack(a_ref, b_ref, dst, scale):
        for pair in range(HEADS // 2):
            cols = slice(pair * B, (pair + 1) * B)
            a, b = a_ref[:, cols], b_ref[:, cols]
            if scale != 1.0:
                a = a * scale
            dst[2 * pair] = jnp.where(low, a, pltpu.roll(b, HD, 1))
            dst[2 * pair + 1] = jnp.where(low, pltpu.roll(a, HD, 1), b)

    loads[0].wait()
    loads[1].wait()
    pack(k_ref, v_ref, kvs, 1.0)
    pl.semaphore_wait(barrier, 62 - 2 * (1 - lax.rem(cw + k, 2)) * (1 - lax.rem(quad + k, 2)))

    def turn(i, n):
        return lax.rem(i + k * (n - 2 * i) + n, n)

    def send_head(src, dst, ssem, rsem, u, j, shared=False):
        h = 3 * u + j
        wk, wz = worker(u, j, shared)
        slot = 8 + lax.rem(z, 4) if shared else z
        me = (wz == z) & (wk == k)

        @pl.when(me)
        def _():
            pltpu.make_async_copy(src.at[h], dst.at[rows(slot * B, B)], rsem.at[slot]).start()

        @pl.when(jnp.logical_not(me))
        def _():
            pltpu.make_async_remote_copy(
                src.at[h], dst.at[rows(slot * B, B)], ssem.at[h], rsem.at[slot],
                device_id=(x * 2 + wk, y * 8 + wz), device_id_type=MESH,
            ).start()

    def send_shared(src, dst, ssem, rsem):
        def step(i, _):
            send_head(src, dst, ssem, rsem, lax.rem(t + turn(i, 4), 4), 1, True)
            return 0

        lax.fori_loop(0, 4, step, 0)

    def send_own(src, dst, ssem, rsem):
        def step(i, _):
            u = lax.rem(t + turn(i, 4), 4)
            for j in (0, 2):
                send_head(src, dst, ssem, rsem, u, j)
            return 0

        lax.fori_loop(0, 4, step, 0)

    def send_own_near(src, dst, ssem, rsem):
        for d in NEAR:
            wz = lax.rem(z + d, 8)
            send_head(src, dst, ssem, rsem, lax.div(wz, 2), 2 * lax.rem(wz, 2))

    def sent_out(src, ssem):
        def step(u, _):
            for j in range(3):
                h = 3 * u + j
                wk, wz = worker(u, j, j == 1)

                @pl.when(jnp.logical_not((wz == z) & (wk == k)))
                def _():
                    pltpu.make_async_copy(src.at[h], src.at[h], ssem.at[h]).wait()
            return 0

        lax.fori_loop(0, 4, step, 0)

    def landed(dst, rsem, slot):
        part = dst.at[rows(slot * B, B)]
        pltpu.make_async_copy(part, part, rsem.at[slot]).wait()

    def send_back(part, dst, ssem, rsem, slot, job):
        oc, oz, h = owner(slot, job)
        me = (oc == k) & (oz == z)

        @pl.when(me)
        def _():
            pltpu.make_async_copy(part, dst.at[h], rsem).start()

        @pl.when(jnp.logical_not(me))
        def _():
            pltpu.make_async_remote_copy(
                part, dst.at[h], ssem.at[slot], rsem,
                device_id=(x * 2 + oc, y * 8 + oz), device_id_type=MESH,
            ).start()

    def sent_back(part, ssem, slot, job):
        oc, oz, _ = owner(slot, job)

        @pl.when(jnp.logical_not((oc == k) & (oz == z)))
        def _():
            pltpu.make_async_copy(part, part, ssem.at[slot]).wait()

    def block(ref, slot):
        return ref.at[rows(slot * B, B)]

    def c3_part(slot, job):
        return u3.at[job, rows(16 * owner(slot, job)[1], 16), :]

    def round_early(what):
        for d in NEAR:
            if d not in LATE:
                what(lax.rem(z + d, 8), 0)

    def both_jobs(what):
        for job, (first, last) in enumerate(((0, 8), (8, 12))):
            def step(i, _, job=job):
                what(i, job)
                return 0

            lax.fori_loop(first, last, step, 0)

    def sibling(m, turned):
        if m == 0:
            return [(0, x, False, flip_y)]
        if m == 1:
            return [(e, x, False, far_y + e) for e in range(2)]
        if m == 2:
            return [(yy, x, True, yy) for yy in range(4)]
        out = []
        for e in range(m - 2):
            for first in range(2):
                xx = flip_x if m == 3 else far_x + e
                out += [(e * 8 + 4 * first + yy, xx, first, yy) for yy in range(4)]
        return out

    def send_subtrees(m, src_part, dst, ssem, rsem, halved=False, jobs=(0, 1)):
        n = B >> m
        for job in jobs:
            c = core_of[job]
            own = m + 5 * job if halved else m
            mine = lax.rem((x * 8 + c * 4 + y), 2**m) * n
            for j, xx, turned, yy in sibling(m, c):
                if m >= 3:
                    index = (j // 8) * 8 + lax.rem(c + (j // 4) % 2, 2) * 4 + j % 4
                else:
                    index = j
                at, count = (k * (n // 2), n // 2) if halved and job == 1 and m < 4 else (0, n)
                pltpu.make_async_remote_copy(
                    src_part(job, index * n + at, count), dst.at[m, job, rows(mine + at, count), :],
                    ssem.at[own], rsem.at[own],
                    device_id=place(job, xx, turned, yy), device_id_type=MESH,
                ).start()

    def wait_all(ref, sem):
        pltpu.make_async_copy(ref, ref, sem).wait()

    send_shared(kvs, kvr, kv_s, kv_r)
    send_own_near(kvs, kvr, kv_s, kv_r)
    loads[2].wait()
    loads[3].wait()
    pack(q_ref, g_ref, qgs, 0.125)
    for start, count in ((C2_A, SETS - C2_A),):
        ga[start * B : (start + count) * B] = jnp.zeros((count * B, B), F32)
    sent_out(kvs, kv_s)
    send_shared(qgs, qgr, qg_s, qg_r)

    def put(index, v):
        h = v.astype(BF16)
        hf = h.astype(F32)
        l = v - hf
        kk = jnp.where(low, hf, pltpu.roll(l, HD, 1))
        vv = jnp.where(low, pltpu.roll(hf, HD, 1), l)
        hl[index, :, 0:B] = kk.astype(BF16)
        hl[index, :, B : 2 * B] = h
        hl[index, :, 2 * B : 3 * B] = vv.astype(BF16)
        hlt[index, 0:B, :] = kk.T.astype(BF16)
        hlt[index, B : 2 * B, :] = vv.T.astype(BF16)

    def halve(ref, start, n):
        return 0.5 * (ref[pl.ds(start, n, stride=2), :] + ref[pl.ds(start + 1, n, stride=2), :])

    for s in range(OWN_B, 12):
        landed(kvr, kv_r, s)
    for i in range(2):
        kvr[(C1_B + i) * B : (C1_B + i + 1) * B] = halve(kvr, (OWN_B + 2 * i) * B, B)
    kvr[30 * B : 31 * B] = halve(kvr, C1_B * B, B)
    c2_mine = kvr.at[pl.ds(30 * B, B)]
    cx = pltpu.make_async_remote_copy(c2_mine, c2o.at[pl.ds(0, B)], cx_s, cx_r, device_id=other, device_id_type=MESH)
    cx.start()
    for s in range(8):
        landed(kvr, kv_r, s)
    for i in range(4):
        kvr[(C1_A + i) * B : (C1_A + i + 1) * B] = halve(kvr, (OWN_A + 2 * i) * B, B)
    for i in range(2):
        kvr[(C2_A + i) * B : (C2_A + i + 1) * B] = halve(kvr, (C1_A + 2 * i) * B, B)
    cs3[0] = halve(kvr, C2_A * B, B)
    cs3[1, rows(64 * k, 64), :] = halve(kvr, 30 * B, 64)
    levels = (cs3, cs4, cs5, cs6, cs7)

    def send_levels(job):
        for m in range(5):
            if m:
                levels[m][job] = halve(levels[m - 1].at[job], 0, B >> m)
            send_subtrees(m, lambda job, at, n: levels[m].at[job], sib, sb_s, sb_r, jobs=(job,))

    send_levels(0)
    cx.wait_recv()
    cs3[1, rows(64 * (1 - k), 64), :] = halve(c2o, 0, 64)
    send_levels(1)
    send_own(qgs, qgr, qg_s, qg_r)

    def put_step(i, _):
        put(i, kvr[rows(i * B, B), :])
        return 0

    lax.fori_loop(0, 20, put_step, 0)
    put(C2_O, c2o[0:B])
    for m in range(5):
        wait_all(sib.at[m], sb_r.at[m])
        put(SIB_B + m, sib[m, 1])

    def load_set(position, index):
        part = slice(position * B, (position + 1) * B)
        xs[part, :] = hl[index]
        xt[:, part] = hlt[index]

    low2 = lax.broadcasted_iota(jnp.int32, (2 * B, B), 1) < HD

    def run_pair(b, job):
        own, c1 = ((OWN_A, C1_A), (OWN_B, C1_B))[job]
        first = own + 2 * b
        side = c1 + flip(b)
        far = C2_A + flip(lax.div(b, 2)) if job == 0 else C2_O
        load_set(0, first)
        load_set(1, first + 1)
        load_set(2, side)
        load_set(3, far)
        landed(qgr, qg_r, first)
        landed(qgr, qg_r, first + 1)
        qg = qgr[rows(first * B, 2 * B), :]
        zero = jnp.zeros_like(qg)

        def halves(v):
            h = v.astype(BF16).astype(F32)
            return h, v - h

        h, l = halves(jnp.where(low2, qg * math.log2(math.e), qg))
        turned = pltpu.roll(h, HD, 1)
        rq = jnp.concatenate([jnp.where(low2, h, turned), jnp.where(low2, l, zero)], axis=1).astype(BF16)
        rg = jnp.concatenate([jnp.where(low2, zero, l), jnp.where(low2, turned, h)], axis=1).astype(BF16)
        sd[...] = dot(xs[:, 0 : 2 * B], rq, NT)
        dp[...] = dot(xs[:, B : 3 * B], rg, NT)
        top = jnp.full((8, 2 * B), -jnp.inf, F32)
        offsets = [float(max(i - 1, 0)) for i in range(9)]
        for i in range(9):
            s = sd[i * B : (i + 1) * B]
            top = jnp.maximum(top, jnp.max(s.reshape(16, 8, 2 * B), axis=0) + offsets[i])
        top = jnp.max(top, axis=0, keepdims=True)
        total = jnp.zeros((8, 2 * B), F32)
        along = jnp.zeros((8, 2 * B), F32)
        for i in range(9):
            part = slice(i * B, (i + 1) * B)
            e = jnp.exp2(sd[part] - (top - offsets[i]))
            sd[part] = e
            total = total + jnp.sum(e.reshape(16, 8, 2 * B), axis=0)
            along = along + jnp.sum((e * dp[part]).reshape(16, 8, 2 * B), axis=0)
        norm = 1.0 / jnp.sum(total, axis=0, keepdims=True)
        row_dot = jnp.sum(along, axis=0, keepdims=True) * norm
        for i in range(9):
            part = slice(i * B, (i + 1) * B)
            prob = sd[part] * norm
            ph[part], plo[part] = split(prob)
            dh[part], dl[part] = split(prob * (dp[part] - row_dot))

        dq = dot(xt[0:B], dh[...])
        dq = dq[0:HD] + dq[HD:B] + dot(xt[0:HD], dl[...])
        at = dot(xt[B : 2 * B], ph[...])
        at = at[0:HD] + at[HD:B] + dot(xt[B : B + HD], plo[...])
        rqa[rows(first * B, 2 * B), :] = jnp.concatenate([dq * 0.125, at], axis=0).T
        for s in range(2):
            send_back(block(rqa, first + s), fqa, rq_s, rq_r, first + s, job)

        h, l = halves(qg)
        rk = jnp.concatenate([jnp.where(low2, h, zero), jnp.where(low2, l, zero)], axis=1).astype(BF16)
        rv = jnp.concatenate([jnp.where(low2, zero, h), jnp.where(low2, zero, l)], axis=1).astype(BF16)
        high = dot(dh[...], rk) + dot(ph[...], rv)
        grads = high[:, 0:B] + high[:, B : 2 * B] + (dot(dl[...], rk[:, 0:B]) + dot(plo[...], rv[:, 0:B]))
        ga[rows(first * B, 2 * B), :] = grads[0 : 2 * B]
        ga[rows(side * B, B), :] = grads[2 * B : 3 * B]
        ga[rows(far * B, B), :] = ga[rows(far * B, B), :] + grads[3 * B : 4 * B]
        top_sets = slice((SIB_A, SIB_B)[job] * B, ((SIB_A, SIB_B)[job] + 5) * B)
        ga[top_sets] = ga[top_sets] + grads[4 * B :]

    def run_job(job, count):
        for m in range(5):
            if job == 0:
                put(SIB_A + m, sib[m, 0])
            load_set(4 + m, (SIB_A, SIB_B)[job] + m)

        def step(i, _):
            run_pair(i if job else lax.rem(t + 4 - turn(i, 4), 4), job)
            return 0

        lax.fori_loop(0, count, step, 0)

    def spread(src, dst, start, n):
        half = 0.5 * src
        for odd in range(2):
            at = pl.ds(start + odd, n, stride=2)
            dst[at, :] = dst[at, :] + half

    run_job(1, 2)
    gx_src = ga.at[pl.ds(C2_O * B, 6 * B)]
    gx = pltpu.make_async_remote_copy(gx_src, xr, gx_s, gx_r, device_id=other, device_id_type=MESH)
    gx.start()
    run_job(0, 4)
    gx.wait()
    for m in range(5):
        gs[m, 0] = ga[(SIB_A + m) * B : (SIB_A + m + 1) * B]
        gs[m, 1] = ga[(SIB_B + m) * B : (SIB_B + m + 1) * B] + xr[(1 + m) * B : (2 + m) * B]
        send_subtrees(m, lambda job, at, n: gs.at[m, job, rows(at, n), :], gr, gs_s, gs_r, True)

    for i in range(2):
        spread(ga[(C2_A + i) * B : (C2_A + i + 1) * B], ga, (C1_A + 2 * i) * B, B)
    for i in range(4):
        spread(ga[(C1_A + i) * B : (C1_A + i + 1) * B], ga, (OWN_A + 2 * i) * B, B)
    spread(xr[0:B], ga, C1_B * B, B)
    for i in range(2):
        spread(ga[(C1_B + i) * B : (C1_B + i + 1) * B], ga, (OWN_B + 2 * i) * B, B)
    def send_now(i, job):
        send_back(block(ga, i), fkv, rk_s, rk_r, i, job)

    round_early(send_now)

    nought[...] = jnp.zeros_like(nought)
    for u in range(4):
        pltpu.make_async_copy(nought, fc3.at[3 * u + 1], rc_r).start()
    for d in LATE:
        wz = lax.rem(z + 8 - d, 8)
        pltpu.make_async_copy(nought, fc3.at[3 * lax.div(wz, 2) + 2 * lax.rem(wz, 2)], rc_r).start()


    def wait_halved(m, sem):
        wait_all(gr.at[m, 0], sem.at[m])
        wait_all(gr.at[m, 1] if m == 4 else gr.at[m, 1, 0:64], sem.at[5 + m])

    ups = (u3, u4, u5, u6, u7)
    for m in (4, 3, 2, 1, 0):
        wait_halved(m, gs_r)
        n = B >> m
        acc = gr[m, 0, 0:n]
        for j in range(1, 2**m):
            acc = acc + gr[m, 0, j * n : (j + 1) * n]
        ups[m][0] = acc
        at, count = (k * (n // 2), n // 2) if m < 4 else (0, n)
        acc = gr[m, 1, rows(at, count), :]
        for j in range(1, 2**m):
            acc = acc + gr[m, 1, rows(j * n + at, count), :]
        if m == 3:
            u6[1] = jnp.zeros((16, B), F32)
        ups[m][1, rows(at, count), :] = acc
    for m in (4, 3, 2, 1):
        n = B >> m
        spread(ups[m][0], ups[m - 1].at[0], 0, n)
        if m == 4:
            spread(u7[1], u6.at[1], 0, n)
        else:
            h = n // 2
            spread(ups[m][1, rows(k * h, h), :], ups[m - 1].at[1], 2 * k * h, h)

    def send_late(i, job):
        above = u3[job, rows(16 * owner(i, job)[1], 16), :] * 0.125
        part = rows(i * B, B)
        ga[part, :] = ga[part, :] + jnp.broadcast_to(above[:, None, :], (16, 8, B)).reshape(B, B)
        send_now(i, job)

    def late_shared(i, _):
        send_late(8 + lax.rem(z + i, 4), 1)
        return 0

    lax.fori_loop(0, 4, late_shared, 0)
    for d in LATE:
        send_late(lax.rem(z + d, 8), 0)
    round_early(lambda i, job: send_back(c3_part(i, job), fc3, rc_s, rc_r, i, job))

    sent_out(qgs, qg_s)
    cx.wait_send()
    for m in range(5):
        wait_all(sib.at[m], sb_s.at[m])
        wait_halved(m, gs_s)
    both_jobs(lambda i, job: sent_back(block(rqa, i), rq_s, i, job))
    wait_all(fqa, rq_r)

    def finish(i, job):
        sent_back(block(ga, i), rk_s, i, job)

    both_jobs(finish)
    round_early(lambda i, job: sent_back(c3_part(i, job), rc_s, i, job))
    wait_all(fkv, rk_r)
    wait_all(fc3, rc_r)


def unpack(qa, kv, c3, oa, oq, ok, ov):
    low = lax.broadcasted_iota(jnp.int32, (B, B), 1) < HD

    def pair(even, odd, first, last):
        first[...] = jnp.where(low, even, pltpu.roll(odd, HD, 1))
        last[...] = jnp.where(low, pltpu.roll(even, HD, 1), odd)

    def whole(h):
        above = jnp.broadcast_to(c3[h][:, None, :] * 0.125, (16, 8, B)).reshape(B, B)
        return kv[h] + above

    for i in range(3):
        cols = slice(i * B, (i + 1) * B)
        pair(qa[2 * i], qa[2 * i + 1], oq.at[:, cols], oa.at[:, cols])
        pair(whole(2 * i), whole(2 * i + 1), ok.at[:, cols], ov.at[:, cols])


def on_device(queries, keys, values, cotangent):
    hbm = pl.BlockSpec(memory_space=pl.ANY)
    dma = pltpu.SemaphoreType.DMA
    scratch = [pltpu.VMEM(queries.shape, F32)] * 4
    scratch += [
        pltpu.VMEM((12, B, B), F32),
        pltpu.VMEM((12, B, B), F32),
        pltpu.VMEM(((SETS + 1) * B, B), F32),
        pltpu.VMEM((12 * B, B), F32),
        pltpu.VMEM((2 * B, B), F32),
    ]
    scratch += [pltpu.VMEM((3, B >> m, B), F32) for m in range(5)]
    scratch += [
        pltpu.VMEM((5, 2, B, B), F32),
        pltpu.VMEM((SETS, B, 3 * B), BF16),
        pltpu.VMEM((SETS, 2 * B, B), BF16),
        pltpu.VMEM((9 * B, 3 * B), BF16),
        pltpu.VMEM((2 * B, 9 * B), BF16),
        pltpu.VMEM((9 * B, 2 * B), F32),
        pltpu.VMEM((9 * B, 2 * B), F32),
    ]
    scratch += [pltpu.VMEM((9 * B, 2 * B), BF16)] * 4
    scratch += [
        pltpu.VMEM((SETS * B, B), F32),
        pltpu.VMEM((6 * B, B), F32),
        pltpu.VMEM((5, 2, B, B), F32),
        pltpu.VMEM((5, 2, B, B), F32),
    ]
    scratch += [pltpu.VMEM((3, B >> m, B), F32) for m in range(5)]
    scratch += [
        pltpu.VMEM((16, B), F32),
        pltpu.VMEM((12 * B, B), F32),
    ]
    scratch += [dma((4,))] + [dma((12,))] * 4 + [dma] * 2 + [dma((5,))] * 2 + [dma] * 2 + [dma((10,))] * 2
    scratch += [dma((12,)), dma] * 3
    packed = pl.pallas_call(
        kernel,
        out_shape=[jax.ShapeDtypeStruct((12, n, B), F32) for n in (B, B, 16)],
        in_specs=[hbm] * 4,
        out_specs=[hbm] * 3,
        scratch_shapes=scratch,
        compiler_params=pltpu.CompilerParams(
            collective_id=0, has_side_effects=True, vmem_limit_bytes=56 * 2**20
        ),
    )(queries, keys, values, cotangent)
    return pl.pallas_call(
        unpack,
        grid=(HEADS // 6,),
        out_shape=[jax.ShapeDtypeStruct(queries.shape, F32)] * 4,
        in_specs=[pl.BlockSpec((6, n, B), lambda i: (i, 0, 0)) for n in (B, B, 16)],
        out_specs=[pl.BlockSpec((B, 3 * B), lambda i: (0, i))] * 4,
    )(*packed)


def solution(mesh):
    spec = P(("seqhi", "seqlo"), None)
    return jax.shard_map(
        on_device, mesh=mesh, in_specs=(spec,) * 4, out_specs=(spec,) * 4, check_vma=False
    )
```
